512 devices in a mesh: ens: 8 (over y_lo, x), slab: 64 (over y_hi, z, core).
Axes of the slice: x: 4, y: 4 (y_hi: 2, y_lo: 2; y = y_hi * 2 + y_lo), z: 16, core: 2. Of those that a mesh axis runs over, the one named last changes fastest.
Arguments:
- state: float32 [64, 64, 1024], P('slab'), may hold values from -6 to 6
- face_coefs: bfloat16 [2, 64, 64, 1024], P(None, 'slab'), may hold values from 0.019897461 to 0.19921875
- codes: int32 [8], P('ens'), may hold values from 0 to 999999
- acoustic_inv: float32 [64, 64, 64], P('slab')
- bounds: int32 [5], replicated, may hold values from 0 to 64, as said below
- land_mask: int32 [64, 1024], P('slab'), may hold values 0 or 1
- target: bfloat16 [64, 64, 1024], P(None, 'slab'), may hold values from -6 to 6
- w_in: bfloat16 [64, 1024], replicated, may hold values from -0.75 to 0.75
- bias_in: float32 [1024], replicated, may hold values from -3 to 3
- land_weight: float32 [1024], replicated, may hold values from -4 to 4
- w_out: bfloat16 [1024, 64], replicated, may hold values from -0.1875 to 0.1875
- bias_out: float32 [64], replicated, may hold values from -3 to 3
Outputs:
- upd_in: float32 [64, 1024], replicated
- upd_out: float32 [1024, 64], replicated
- grad_state: float32 [64, 64, 1024], P('slab')
The draws below stay inside these ranges and needn't reach their ends.
Inputs may be any that keep to these rules, and one draw needn't show every extreme that they name: bounds[0] = 0 and bounds[4] = 64; the entries rise strictly.
All inputs are finite; a program needn't handle non-finite values. No bound on the sum of `land_mask` on one device may be relied on, other than what follows from the above.
Results may differ from the reference program's by a relative error of at most 0.0004.
The reference program's roundings to bfloat16 on the way count: a program that leaves them out, or rounds other values in their place, can miss the bound.
Values sent between devices are 32-bit elements; how exact they have to be, the bound alone decides.
A program may use at most 64 MiB of HBM per device.

```python
import math
import jax
import jax.numpy as jnp
from jax import lax

NLEV = 64
HID = 1024
NBLK = 4
NLON = 1024
MEMBERS = 8
NLAT = 64


def draw_acoustic_inv(key, part):
    first, second = jax.random.split(key)
    diag = jax.random.uniform(first, (NLAT, NLEV), jnp.float32, 1.0, 2.0)
    off = jax.random.uniform(second, (NLAT, NLEV, NLEV), jnp.float32, -1.0, 1.0) * (1.2 / NLEV ** 0.5)
    eye = jnp.eye(NLEV, dtype=jnp.float32)
    return off * (1.0 - eye)[None] + diag[:, :, None] * eye[None]


def draw_bounds(key, part):
    inner = jax.random.permutation(key, NLEV - 1)[:NBLK - 1] + 1
    inner = jnp.sort(inner).astype(jnp.int32)
    return jnp.concatenate([jnp.zeros((1,), jnp.int32), inner, jnp.full((1,), NLEV, jnp.int32)])


def place_ends(values, own_key, smallest, high):
    dims = values.shape
    spot = [jax.random.randint(jax.random.fold_in(own_key, axis), (), 0, dims[axis]) for axis in range(len(dims))]
    values = values.at[tuple(spot)].set(smallest)
    longest = dims.index(max(dims))
    spot[longest] = (spot[longest] + 1) % dims[longest]
    return values.at[tuple(spot)].set(high)


def shard_levels(stream_key, extent, shards, low, top_value):
    gain = 1.0
    for dim, shards_of in shards:
        draws = jax.random.uniform(jax.random.fold_in(jax.random.fold_in(stream_key, 6), dim), (shards_of,), jnp.float32, low / len(shards), top_value / len(shards))
        gain = gain * jnp.repeat(jnp.exp(draws), extent[dim] // shards_of).reshape((-1,) + (1,) * (len(extent) - 1 - dim))
    return gain


def normal_values(stream_key, dims, scale, most, pieces=(), kind=jnp.bfloat16):
    gain = shard_levels(stream_key, dims, pieces, -0.22, 0.18) if pieces else 1.0
    entries = jax.random.normal(stream_key, dims, jnp.float32) * scale * gain
    return jnp.minimum(jnp.maximum(entries, -most), most).astype(kind)


def setup_inputs(seed: int = 0) -> dict:
    streams_of = jax.random.split(jax.random.key(seed), 13)
    state = normal_values(streams_of[0], (NLEV, NLAT, NLON), 1.0, 6.0, ((0, 64),), jnp.float32)
    face_coefs = jnp.clip(jnp.exp(math.log(0.19921875) - 2.3038113 * jax.random.uniform(streams_of[1], (2, NLEV, NLAT, NLON), jnp.float32) ** shard_levels(streams_of[1], (2, NLEV, NLAT, NLON), ((1, 64),), -0.2, 0.2)), 0.019897461, 0.19921875).astype(jnp.bfloat16)
    codes = place_ends(jax.random.randint(streams_of[2], (MEMBERS,), 0, 1000000), jax.random.fold_in(streams_of[2], 1), 0, 999999).astype(jnp.int32)
    acoustic_inv = draw_acoustic_inv(jax.random.fold_in(streams_of[12], 71), 0)
    bounds = draw_bounds(jax.random.fold_in(streams_of[12], 71), 0)
    land_mask = place_ends((jax.random.randint(streams_of[5], (NLAT, NLON), 0, 10) < 3).astype(jnp.int32), jax.random.fold_in(streams_of[5], 1), 0, 1)
    target = normal_values(streams_of[6], (NLEV, NLAT, NLON), 1.0, 6.0, ((1, 64),))
    w_in = normal_values(streams_of[7], (NLEV, HID), NLEV ** -0.5, 0.75)
    bias_in = normal_values(streams_of[8], (HID,), 0.5, 3.0, (), jnp.float32)
    land_weight = normal_values(streams_of[9], (HID,), 0.8, 4.0, (), jnp.float32)
    w_out = normal_values(streams_of[10], (HID, NLEV), HID ** -0.5, 0.1875)
    bias_out = normal_values(streams_of[11], (NLEV,), 0.5, 3.0, (), jnp.float32)
    return dict(state=state, face_coefs=face_coefs, codes=codes, acoustic_inv=acoustic_inv, bounds=bounds, land_mask=land_mask, target=target, w_in=w_in, bias_in=bias_in, land_weight=land_weight, w_out=w_out, bias_out=bias_out)


def noise(code, cell):
    mult = code % 251 + 2
    first = (mult * (cell % 65521) + 12345) % 65521
    second = (first * 31337 + mult) % 65521
    return second.astype(jnp.float32) / 65521.0 - 0.5

def diffuse(field, east, north):
    flux_x = east * (jnp.roll(field, -1, axis=2) - field)
    step_y = jnp.concatenate([field[:, 1:] - field[:, :-1], jnp.zeros_like(field[:, :1])], axis=1)
    flux_y = north * step_y
    lower = jnp.concatenate([jnp.zeros_like(flux_y[:, :1]), flux_y[:, :-1]], axis=1)
    return field + flux_x - jnp.roll(flux_x, 1, axis=2) + flux_y - lower

def column_step(x_row, land_row, target_row, solve_row, w_in, bias_in, land_weight, w_out, bias_out, scale):
    pre = lax.dot_general(w_in, x_row, (((0,), (0,)), ((), ())), preferred_element_type=jnp.float32)
    pre = pre + bias_in[:, None] + land_weight[:, None] * land_row[None, :]
    sig = jax.nn.sigmoid(pre)
    hidden = (pre * sig).astype(jnp.bfloat16)
    out = lax.dot_general(w_out, hidden, (((0,), (0,)), ((), ())), preferred_element_type=jnp.float32)
    out = out + bias_out[:, None]
    d_out = ((out - target_row.astype(jnp.float32)) * scale).astype(jnp.bfloat16)
    g_out = lax.dot_general(hidden, d_out, (((1,), (1,)), ((), ())), preferred_element_type=jnp.float32)
    d_hidden = jnp.dot(w_out, d_out, preferred_element_type=jnp.float32)
    d_pre = (d_hidden * sig * (1.0 + pre * (1.0 - sig))).astype(jnp.bfloat16)
    g_in = lax.dot_general(x_row, d_pre, (((1,), (1,)), ((), ())), preferred_element_type=jnp.float32)
    d_x = jnp.dot(w_in, d_pre, preferred_element_type=jnp.float32)
    d_h = lax.dot_general(solve_row, d_x, (((0,), (0,)), ((), ())), precision=lax.Precision.HIGHEST)
    return (g_in, g_out, d_h)

def coupling(acoustic_inv, bounds, nlev, nblk):
    level = jnp.arange(nlev, dtype=jnp.int32)
    block = lax.optimization_barrier(jnp.sum((level[:, None] >= bounds[None, 1:nblk]).astype(jnp.int32), axis=1))
    couple = (block[:, None] == block[None, :]).astype(jnp.float32)
    return acoustic_inv * couple[None]

def normalized(grad):
    return grad / jnp.sqrt(jnp.mean(grad * grad) + 1e-06)

def reference(state, face_coefs, codes, acoustic_inv, bounds, land_mask, target, w_in, bias_in, land_weight, w_out, bias_out):
    east = face_coefs[0].astype(jnp.float32)
    north = face_coefs[1].astype(jnp.float32)
    solve_mat = coupling(acoustic_inv, bounds, NLEV, NBLK)
    cell = jnp.arange(NLEV * NLAT * NLON, dtype=jnp.int32).reshape(NLEV, NLAT, NLON)
    land = land_mask.astype(jnp.float32)
    scale = 1.0 / MEMBERS

    def member(carry, code):
        g_in, g_out, back = carry
        fresh = diffuse(state + noise(code, cell), east, north)
        solved = jnp.einsum('jlk,kji->jli', solve_mat, fresh, precision=lax.Precision.HIGHEST).astype(jnp.bfloat16)

        def per_row(inner, row):
            acc_in, acc_out = inner
            x_row = lax.dynamic_index_in_dim(solved, row, 0, keepdims=False)
            land_row = lax.dynamic_index_in_dim(land, row, 0, keepdims=False)
            target_row = lax.dynamic_index_in_dim(target, row, 1, keepdims=False)
            solve_row = lax.dynamic_index_in_dim(solve_mat, row, 0, keepdims=False)
            part_in, part_out, d_h = column_step(x_row, land_row, target_row, solve_row, w_in, bias_in, land_weight, w_out, bias_out, scale)
            return ((acc_in + part_in, acc_out + part_out), d_h)
        (g_in, g_out), d_rows = lax.scan(per_row, (g_in, g_out), jnp.arange(NLAT, dtype=jnp.int32))
        return ((g_in, g_out, back + d_rows), None)
    start = (jnp.zeros((NLEV, HID), jnp.float32), jnp.zeros((HID, NLEV), jnp.float32), jnp.zeros((NLAT, NLEV, NLON), jnp.float32))
    (g_in, g_out, back), _ = lax.scan(member, start, codes)
    summed = jnp.transpose(back, (1, 0, 2))
    grad_state = diffuse(summed, east, north)
    return (normalized(g_in), normalized(g_out), grad_state)
```

```python
import functools

import jax
import jax.numpy as jnp
from jax import lax
from jax.experimental import pallas as pl
from jax.experimental.pallas import tpu as pltpu
from jax.sharding import PartitionSpec as P

MESH = pl.DeviceIdType.MESH
LANES = 128
PRIME = 65521


def reduced(value):
    value = (value & 65535) + 15 * (value >> 16)
    return value


def below_prime(value):
    return jnp.where(value >= PRIME, value - PRIME, value)


def noise(mult, base, first_row, rows, lons):
    shape = (rows, lons)
    row = lax.broadcasted_iota(jnp.int32, shape, 0) + first_row
    cell = below_prime(row * lons + lax.broadcasted_iota(jnp.int32, shape, 1) + base)
    first = below_prime(reduced(mult * cell + 12345))
    second = below_prime(reduced(reduced(first * 31337 + mult)))
    return second.astype(jnp.float32) * (1.0 / PRIME) - 0.5


def prepare_north(coef_ref, north):
    lats, lons = coef_ref.shape[1:]
    north[0:8, :] = jnp.zeros((8, lons), jnp.float32)
    for start in range(0, lats, 16):
        part = coef_ref[1, start : start + 16, :].astype(jnp.float32)
        if start + 16 >= lats:
            row = lax.broadcasted_iota(jnp.int32, part.shape, 0) + start
            part = jnp.where(row < lats - 1, part, 0.0)
        north[8 + start : 8 + start + part.shape[0], :] = part


def diffuse(field, coef_ref, north, emit):
    lats, lons = coef_ref.shape[1:]
    step = min(16, lats)
    for start in range(0, lats, step):
        here = field[8 + start : 8 + start + step, :]
        ahead = field[9 + start : 9 + start + step, :]
        behind = field[7 + start : 7 + start + step, :]
        east = coef_ref[0, start : start + step, :].astype(jnp.float32)
        flux_x = east * (pltpu.roll(here, lons - 1, 1) - here)
        flux_y = north[8 + start : 8 + start + step, :] * (ahead - here)
        lower = north[7 + start : 7 + start + step, :] * (here - behind)
        emit(start, step, here + flux_x - pltpu.roll(flux_x, 1, 1) + flux_y - lower)


def offset_of(step, count):
    half = step // 2 + 1
    return jnp.where(step % 2 == 0, half, count - half)


def for_peers(count, me, body):
    def one(step, carry):
        body(lax.rem(me + offset_of(step, count), count))
        return carry

    lax.fori_loop(0, count - 1, one, 0)


def wait_bytes(ref, sem):
    pltpu.make_async_copy(ref, ref, sem).wait()


def rows_of(index, size):
    return pl.ds(pl.multiple_of(index * size, size), size)


def spread_kernel(
    members, slabs, state_ref, coef_ref, code_ref, out_ref, field, north, send, recv, send_sem, recv_sem
):
    ens, slab = lax.axis_index("ens"), lax.axis_index("slab")
    lats, lons = state_ref.shape
    blocks = lons // LANES
    barrier = pltpu.get_barrier_semaphore()
    for_peers(
        slabs,
        slab,
        lambda d: pl.semaphore_signal(barrier, inc=1, device_id=(ens, d), device_id_type=MESH),
    )
    mult = lax.rem(code_ref[0], 251) + 2
    base = lax.rem(slab * (lats * lons), PRIME)
    field[0:8, :] = jnp.zeros((8, lons), jnp.float32)
    field[8 + lats : 16 + lats, :] = jnp.zeros((8, lons), jnp.float32)
    for start in range(0, lats, 8):
        field[8 + start : 16 + start, :] = state_ref[start : start + 8, :] + noise(
            mult, base, start, 8, lons
        )
    prepare_north(coef_ref, north)

    def emit(start, rows, value):
        for j in range(blocks):
            send[pl.ds(start * blocks + j, rows, stride=blocks), :] = value[
                :, j * LANES : (j + 1) * LANES
            ]

    diffuse(field, coef_ref, north, emit)
    pl.semaphore_wait(barrier, slabs - 1)

    def put(d):
        pltpu.make_async_remote_copy(
            src_ref=send.at[rows_of(d, blocks)],
            dst_ref=recv.at[rows_of(slab, blocks)],
            send_sem=send_sem,
            recv_sem=recv_sem,
            device_id=(ens, d),
            device_id_type=MESH,
        ).start()

    for_peers(slabs, slab, put)
    recv[rows_of(slab, blocks), :] = send[rows_of(slab, blocks), :]
    others = pl.ds(0, (slabs - 1) * blocks)
    wait_bytes(recv.at[others], recv_sem)
    out_ref[...] = recv[...]
    wait_bytes(send.at[others], send_sem)


def parts_of(value):
    high = value.astype(jnp.bfloat16).astype(jnp.float32)
    rest = value - high
    middle = rest.astype(jnp.bfloat16).astype(jnp.float32)
    return high, middle, rest - middle


def contract(a, b, dims, **kw):
    return lax.dot_general(a, b, (dims, ((), ())), preferred_element_type=jnp.float32, **kw)


def network_kernel(
    members,
    cols_ref,
    solve_ref,
    bounds_ref,
    land_ref,
    target_ref,
    w_in_ref,
    bias_in_ref,
    land_weight_ref,
    w_out_ref,
    bias_out_ref,
    back_ref,
    grads_ref,
    w_aug,
    w_back,
    x_aug,
    shift,
    z_s,
    slope,
    dy_s,
    da_s,
):
    levels, lons = target_ref.shape
    hidden = w_in_ref.shape[1]
    blocks = lons // LANES
    pad = w_aug.shape[1]
    hb = min(128, hidden)
    cb = min(256, lons)
    row = lax.broadcasted_iota(jnp.int32, (levels, levels), 0)
    col = lax.broadcasted_iota(jnp.int32, (levels, levels), 1)
    row_block = jnp.zeros((levels, levels), jnp.int32)
    col_block = jnp.zeros((levels, levels), jnp.int32)
    for j in range(1, bounds_ref.shape[0] - 1):
        row_block += (row >= bounds_ref[j]).astype(jnp.int32)
        col_block += (col >= bounds_ref[j]).astype(jnp.int32)
    solve = jnp.where(row_block == col_block, solve_ref[...], 0.0)
    bias = parts_of(bias_in_ref[...] * 0.5)
    land_w = parts_of(land_weight_ref[...] * 0.5)
    land = land_ref[...].astype(jnp.float32)
    extra = pad - levels
    extra_row = lax.broadcasted_iota(jnp.int32, (extra, hidden), 0)
    tail = jnp.zeros((extra, hidden), jnp.float32)
    for k, part in enumerate(bias + land_w):
        tail = jnp.where(extra_row == k, part, tail)
    whole = jnp.concatenate([w_in_ref[...].astype(jnp.float32) * 0.5, tail], axis=0)
    w_aug[...] = whole.T.astype(jnp.bfloat16)
    spread = jnp.concatenate(
        [w_out_ref[...].astype(jnp.float32) * 0.5, jnp.zeros((extra, hidden), jnp.float32)], axis=0
    )
    w_back[...] = spread.T.astype(jnp.bfloat16)
    lon_row = lax.broadcasted_iota(jnp.int32, (extra, lons), 0)
    ones = jnp.where(lon_row < 3, 1.0, jnp.where(lon_row < 6, land, 0.0))
    x_aug[levels:, :] = ones.astype(jnp.bfloat16)
    bias_col = jnp.sum(jnp.where(row == col, bias_out_ref[...], 0.0), axis=1, keepdims=True)
    shift[...] = bias_col - target_ref[...].astype(jnp.float32)
    dy_s[levels:, :] = jnp.zeros((extra, lons), jnp.bfloat16)
    highest = lax.Precision.HIGHEST
    for start in range(0, lons, cb):
        here = slice(start, start + cb)
        h = jnp.concatenate(
            [
                cols_ref[pl.ds(j, levels, stride=blocks), :]
                for j in range(start // LANES, (start + cb) // LANES)
            ],
            axis=1,
        )
        x = contract(solve, h, ((1,), (0,)), precision=highest).astype(jnp.bfloat16)
        x_aug[0:levels, here] = x
        x_all = x_aug[:, here]
        for k in range(0, hidden, hb):
            half = contract(w_aug[k : k + hb, :], x_all, ((1,), (0,)))
            t = jnp.tanh(half)
            both = half * t
            z_s[k : k + hb, here] = (half + both).astype(jnp.bfloat16)
            slope[k : k + hb, here] = (1.0 + t) * (1.0 + half - both)
        out = contract(w_out_ref[...], z_s[:, here], ((1,), (0,)))
        dy = ((out + shift[:, here]) * (1.0 / members)).astype(jnp.bfloat16)
        dy_s[0:levels, here] = dy
        dy_all = dy_s[:, here]
        for k in range(0, hidden, hb):
            dz = contract(w_back[k : k + hb, :], dy_all, ((1,), (0,)))
            da_s[k : k + hb, here] = (dz * slope[k : k + hb, here]).astype(jnp.bfloat16)
        dx = contract(w_in_ref[...], da_s[:, here], ((1,), (0,)))
        dh = contract(solve, dx, ((0,), (0,)), precision=highest)
        for j in range(cb // LANES):
            first = (start // LANES + j) * levels
            back_ref[first : first + levels, :] = dh[:, j * LANES : (j + 1) * LANES]
    grads_ref[0] = contract(x_aug[0:levels, :], da_s[...], ((1,), (1,)))
    grads_ref[1] = contract(dy_s[0:levels, :], z_s[...], ((1,), (1,)))


def reduce_kernel(
    members,
    slabs,
    back_ref,
    grads_ref,
    field_ref,
    total_ref,
    back_in,
    pair_in,
    pair_sum,
    grad_in,
    level_out,
    level_in,
    piece_out,
    piece_in,
    piece_sum,
    piece_all,
    field_in,
    rows_out,
    rows_all,
    pair_all,
    send_sem,
    recv_sem,
):
    ens, slab = lax.axis_index("ens"), lax.axis_index("slab")
    core, place = lax.rem(slab, 2), slab // 2
    twin = slab + 1 - 2 * core
    places = slabs // 2
    levels, lons = grads_ref.shape[1:]
    chunk = back_ref.shape[0] // members
    rows = levels // members
    barrier = pltpu.get_barrier_semaphore()

    def greet(device):
        pl.semaphore_signal(barrier, inc=1, device_id=device, device_id_type=MESH)

    for_peers(members, ens, lambda e: greet((e, slab)))
    for_peers(slabs, slab, lambda d: greet((ens, d)))

    def put(k, src, dst, device):
        pltpu.make_async_remote_copy(
            src_ref=src,
            dst_ref=dst,
            send_sem=send_sem.at[k],
            recv_sem=recv_sem.at[k],
            device_id=device,
            device_id_type=MESH,
        ).start()

    pl.semaphore_wait(barrier, members + slabs - 2)
    put(0, grads_ref.at[1 - core], pair_in, (ens, twin))
    for_peers(
        members,
        ens,
        lambda e: put(
            1, back_ref.at[rows_of(e, chunk)], back_in.at[rows_of(ens, chunk)], (e, slab)
        ),
    )
    back_in[rows_of(ens, chunk), :] = back_ref[rows_of(ens, chunk), :]
    wait_bytes(pair_in, recv_sem.at[0])
    pair_sum[...] = grads_ref[core] + pair_in[...]
    for_peers(
        members,
        ens,
        lambda e: put(
            2, pair_sum.at[rows_of(e, rows)], grad_in.at[rows_of(ens, rows)], (e, slab)
        ),
    )
    grad_in[rows_of(ens, rows), :] = pair_sum[rows_of(ens, rows), :]
    wait_bytes(back_in.at[pl.ds(0, (members - 1) * chunk)], recv_sem.at[1])
    total = back_in[0:chunk, :]
    for e in range(1, members):
        total += back_in[e * chunk : (e + 1) * chunk, :]
    for l in range(levels):
        level_out[l] = total[l : l + 1, :]
    for_peers(
        slabs, slab, lambda d: put(3, level_out.at[d], level_in.at[slab], (ens, d))
    )
    level_in[slab] = level_out[slab]
    wait_bytes(grad_in.at[pl.ds(0, (members - 1) * rows)], recv_sem.at[2])
    total = grad_in[0:rows, :]
    for e in range(1, members):
        total += grad_in[e * rows : (e + 1) * rows, :]
    per = rows // 2
    for p in range(places):
        t, s = p // per, p % per
        piece_out[p] = total[2 * s : 2 * s + 2, t * LANES : (t + 1) * LANES]
    for_peers(
        places,
        place,
        lambda q: put(4, piece_out.at[q], piece_in.at[place], (ens, 2 * q + core)),
    )
    piece_in[place] = piece_out[place]
    wait_bytes(level_in.at[pl.ds(0, slabs - 1)], recv_sem.at[3])
    for_peers(members, ens, lambda e: put(5, level_in, field_in.at[ens], (e, slab)))
    field_in[ens] = level_in[...]
    wait_bytes(piece_in.at[pl.ds(0, places - 1)], recv_sem.at[4])
    piece_sum[...] = jnp.sum(piece_in[...], axis=0)
    for_peers(
        places,
        place,
        lambda q: put(6, piece_sum, piece_all.at[place], (ens, 2 * q + core)),
    )
    piece_all[place] = piece_sum[...]
    wait_bytes(piece_all.at[pl.ds(0, places - 1)], recv_sem.at[6])
    for p in range(places):
        t, s = p // per, p % per
        rows_out[2 * s : 2 * s + 2, t * LANES : (t + 1) * LANES] = piece_all[p]
    for_peers(
        members, ens, lambda e: put(7, rows_out, rows_all.at[rows_of(ens, rows)], (e, slab))
    )
    rows_all[rows_of(ens, rows), :] = rows_out[...]
    wait_bytes(rows_all.at[pl.ds(0, (members - 1) * rows)], recv_sem.at[7])
    put(8, rows_all, pair_all, (ens, twin))
    total_ref[core] = rows_all[...]
    wait_bytes(field_in.at[pl.ds(0, members - 1)], recv_sem.at[5])
    for e in range(members):
        field_ref[e] = field_in[e].reshape(levels, LANES)
    wait_bytes(pair_all, recv_sem.at[8])
    total_ref[1 - core] = pair_all[...]
    wait_bytes(grads_ref.at[0], send_sem.at[0])
    wait_bytes(back_in.at[pl.ds(0, (members - 1) * chunk)], send_sem.at[1])
    wait_bytes(grad_in.at[pl.ds(0, (members - 1) * rows)], send_sem.at[2])
    wait_bytes(level_in.at[pl.ds(0, slabs - 1)], send_sem.at[3])
    wait_bytes(piece_in.at[pl.ds(0, places - 1)], send_sem.at[4])
    wait_bytes(field_in.at[pl.ds(0, members - 1)], send_sem.at[5])
    wait_bytes(piece_all.at[pl.ds(0, places - 1)], send_sem.at[6])
    wait_bytes(rows_all.at[pl.ds(0, (members - 1) * rows)], send_sem.at[7])
    wait_bytes(pair_all, send_sem.at[8])


def finish_kernel(field_ref, total_ref, coef_ref, in_ref, out_ref, state_ref, field, north):
    lats, lons = state_ref.shape
    for k, ref in ((0, in_ref), (1, out_ref)):
        grad = total_ref[k]
        square = jnp.sum(jnp.sum(grad * grad, axis=0, keepdims=True), axis=1, keepdims=True)
        ref[...] = grad / jnp.sqrt(square * (1.0 / grad.size) + 1e-06)
    field[0:8, :] = jnp.zeros((8, lons), jnp.float32)
    field[8 + lats : 16 + lats, :] = jnp.zeros((8, lons), jnp.float32)
    for j in range(field_ref.shape[0]):
        field[8 : 8 + lats, j * LANES : (j + 1) * LANES] = field_ref[j]
    prepare_north(coef_ref, north)

    def emit(start, rows, value):
        state_ref[start : start + rows, :] = value

    diffuse(field, coef_ref, north, emit)


def on_device(
    members,
    slabs,
    state,
    face_coefs,
    codes,
    acoustic_inv,
    bounds,
    land_mask,
    target,
    w_in,
    bias_in,
    land_weight,
    w_out,
    bias_out,
):
    _, lats, lons = state.shape
    levels, hidden = w_in.shape
    blocks = lons // LANES
    f32, bf16 = jnp.float32, jnp.bfloat16
    vmem = pl.BlockSpec(memory_space=pltpu.VMEM)
    smem = pl.BlockSpec(memory_space=pltpu.SMEM)
    like = jax.ShapeDtypeStruct
    dma = pltpu.SemaphoreType.DMA
    coefs = face_coefs.reshape(2, lats, lons)
    limit = 40 * 1024 * 1024
    columns = pl.pallas_call(
        functools.partial(spread_kernel, members, slabs),
        out_shape=like((levels * blocks, LANES), f32),
        in_specs=[vmem, vmem, smem],
        out_specs=vmem,
        scratch_shapes=[
            pltpu.VMEM((lats + 16, lons), f32),
            pltpu.VMEM((lats + 8, lons), f32),
            pltpu.VMEM((lats * blocks, LANES), f32),
            pltpu.VMEM((levels * blocks, LANES), f32),
            dma,
            dma,
        ],
        compiler_params=pltpu.CompilerParams(
            collective_id=0, has_side_effects=True, vmem_limit_bytes=limit
        ),
    )(state.reshape(lats, lons), coefs, codes)
    pad = 2 * levels if levels >= 64 else levels + 8
    back, grads = pl.pallas_call(
        functools.partial(network_kernel, members),
        out_shape=(like((blocks * levels, LANES), f32), like((2, levels, hidden), f32)),
        in_specs=[vmem, vmem, smem] + [vmem] * 7,
        out_specs=(vmem, vmem),
        scratch_shapes=[
            pltpu.VMEM((hidden, pad), bf16),
            pltpu.VMEM((hidden, pad), bf16),
            pltpu.VMEM((pad, lons), bf16),
            pltpu.VMEM((levels, lons), f32),
            pltpu.VMEM((hidden, lons), bf16),
            pltpu.VMEM((hidden, lons), f32),
            pltpu.VMEM((pad, lons), bf16),
            pltpu.VMEM((hidden, lons), bf16),
        ],
        compiler_params=pltpu.CompilerParams(vmem_limit_bytes=limit),
    )(
        columns,
        acoustic_inv.reshape(levels, levels),
        bounds,
        land_mask,
        target.reshape(levels, lons),
        w_in,
        bias_in.reshape(1, hidden),
        land_weight.reshape(1, hidden),
        w_out.T,
        bias_out.reshape(1, levels),
    )
    rows = levels // members
    places = slabs // 2
    chunk = levels * blocks // members
    field, total = pl.pallas_call(
        functools.partial(reduce_kernel, members, slabs),
        out_shape=(like((members, levels, LANES), f32), like((2, levels, hidden), f32)),
        in_specs=[vmem, vmem],
        out_specs=(vmem, vmem),
        scratch_shapes=[
            pltpu.VMEM((members * chunk, LANES), f32),
            pltpu.VMEM((levels, hidden), f32),
            pltpu.VMEM((levels, hidden), f32),
            pltpu.VMEM((levels, hidden), f32),
            pltpu.VMEM((levels, 1, LANES), f32),
            pltpu.VMEM((levels, 1, LANES), f32),
            pltpu.VMEM((places, 2, LANES), f32),
            pltpu.VMEM((places, 2, LANES), f32),
            pltpu.VMEM((2, LANES), f32),
            pltpu.VMEM((places, 2, LANES), f32),
            pltpu.VMEM((members, levels, 1, LANES), f32),
            pltpu.VMEM((rows, hidden), f32),
            pltpu.VMEM((levels, hidden), f32),
            pltpu.VMEM((levels, hidden), f32),
            dma((9,)),
            dma((9,)),
        ],
        compiler_params=pltpu.CompilerParams(
            collective_id=1, has_side_effects=True, vmem_limit_bytes=limit
        ),
    )(back, grads)
    upd_in, upd_out, grad_state = pl.pallas_call(
        finish_kernel,
        out_shape=(
            like((levels, hidden), f32),
            like((levels, hidden), f32),
            like((lats, lons), f32),
        ),
        in_specs=[vmem] * 3,
        out_specs=(vmem,) * 3,
        scratch_shapes=[
            pltpu.VMEM((lats + 16, lons), f32),
            pltpu.VMEM((lats + 8, lons), f32),
        ],
        compiler_params=pltpu.CompilerParams(vmem_limit_bytes=limit),
    )(field, total, coefs)
    return upd_in, upd_out.T, grad_state.reshape(state.shape)


def solution(mesh):
    placed = (
        P("slab", None, None),
        P(None, "slab", None, None),
        P("ens"),
        P("slab", None, None),
        P(),
        P("slab", None),
        P(None, "slab", None),
        P(),
        P(),
        P(),
        P(),
        P(),
    )
    return jax.shard_map(
        functools.partial(on_device, mesh.shape["ens"], mesh.shape["slab"]),
        mesh=mesh,
        in_specs=placed,
        out_specs=(P(), P(), P("slab", None, None)),
        check_vma=False,
    )
```

```python
import functools

import jax
import jax.numpy as jnp
from jax import lax
from jax.experimental import pallas as pl
from jax.experimental.pallas import tpu as pltpu
from jax.sharding import PartitionSpec as P

MESH = pl.DeviceIdType.MESH
LANES = 128
PRIME = 65521


def reduced(value):
    value = (value & 65535) + 15 * (value >> 16)
    return value


def below_prime(value):
    return jnp.where(value >= PRIME, value - PRIME, value)


def noise(mult, base, first_row, rows, lons):
    shape = (rows, lons)
    row = lax.broadcasted_iota(jnp.int32, shape, 0) + first_row
    cell = below_prime(row * lons + lax.broadcasted_iota(jnp.int32, shape, 1) + base)
    first = below_prime(reduced(mult * cell + 12345))
    second = below_prime(reduced(reduced(first * 31337 + mult)))
    return second.astype(jnp.float32) * (1.0 / PRIME) - 0.5


def prepare_north(coef_ref, north):
    lats, lons = coef_ref.shape[1:]
    north[0:8, :] = jnp.zeros((8, lons), jnp.float32)
    for start in range(0, lats, 16):
        part = coef_ref[1, start : start + 16, :].astype(jnp.float32)
        if start + 16 >= lats:
            row = lax.broadcasted_iota(jnp.int32, part.shape, 0) + start
            part = jnp.where(row < lats - 1, part, 0.0)
        north[8 + start : 8 + start + part.shape[0], :] = part


def diffuse(field, coef_ref, north, emit):
    lats, lons = coef_ref.shape[1:]
    step = min(16, lats)
    for start in range(0, lats, step):
        here = field[8 + start : 8 + start + step, :]
        ahead = field[9 + start : 9 + start + step, :]
        behind = field[7 + start : 7 + start + step, :]
        east = coef_ref[0, start : start + step, :].astype(jnp.float32)
        flux_x = east * (pltpu.roll(here, lons - 1, 1) - here)
        flux_y = north[8 + start : 8 + start + step, :] * (ahead - here)
        lower = north[7 + start : 7 + start + step, :] * (here - behind)
        emit(start, step, here + flux_x - pltpu.roll(flux_x, 1, 1) + flux_y - lower)


def offset_of(step, count):
    half = step // 2 + 1
    return jnp.where(step % 2 == 0, half, count - half)


def for_peers(count, me, body):
    def one(step, carry):
        body(lax.rem(me + offset_of(step, count), count))
        return carry

    lax.fori_loop(0, count - 1, one, 0)


def wait_bytes(ref, sem):
    pltpu.make_async_copy(ref, ref, sem).wait()


def rows_of(index, size):
    return pl.ds(pl.multiple_of(index * size, size), size)


def parts_of(value):
    high = value.astype(jnp.bfloat16).astype(jnp.float32)
    rest = value - high
    middle = rest.astype(jnp.bfloat16).astype(jnp.float32)
    return high, middle, rest - middle


def contract(a, b, dims, **kw):
    return lax.dot_general(a, b, (dims, ((), ())), preferred_element_type=jnp.float32, **kw)


def step_kernel(
    members,
    slabs,
    state_hbm,
    coef_hbm,
    solve_hbm,
    land_hbm,
    target_hbm,
    w_in_hbm,
    bias_in_hbm,
    land_weight_hbm,
    w_out_hbm,
    bias_out_hbm,
    code_ref,
    bounds_ref,
    state_ref,
    total_ref,
    state_in,
    coef_ref,
    solve_ref,
    land_ref,
    target_ref,
    w_in_ref,
    bias_in_ref,
    land_weight_ref,
    w_out_ref,
    bias_out_ref,
    field,
    north,
    send,
    recv,
    solve_s,
    w_aug,
    w_back,
    x_aug,
    shift,
    z_s,
    slope,
    dy_s,
    da_s,
    back,
    back_in,
    grads,
    pair_in,
    pair_sum,
    plane_in,
    near_in,
    far_in,
    piece,
    level_out,
    level_in,
    field_in,
    half_all,
    twin_all,
    load_sem,
    chunk_sem,
    send_sem,
    recv_sem,
):
    ens, slab = lax.axis_index("ens"), lax.axis_index("slab")
    lats, lons = state_in.shape
    levels, hidden = w_in_ref.shape
    blocks = lons // LANES
    chunks, pad, width = x_aug.shape
    wide = width // LANES
    extra = pad - levels
    hb = min(128, hidden)
    core = lax.rem(slab, 2)
    twin = slab + 1 - 2 * core
    half_slabs = slabs // 2
    upper = slab // half_slabs
    other = lax.rem(slab + half_slabs, slabs)
    column = lax.rem(slab, half_slabs)
    near = near_in.shape[0] // piece.shape[0]
    far = far_in.shape[0] // piece.shape[0]
    heights = near * far
    height = column // 2
    plane = ens * 2 + upper
    planes = members * 2
    rows = piece.shape[0]
    half = hidden // 2
    highest = lax.Precision.HIGHEST

    loads = [
        pltpu.make_async_copy(src, dst, load_sem.at[k])
        for k, (src, dst) in enumerate(
            (
                (state_hbm, state_in),
                (coef_hbm, coef_ref),
                (solve_hbm, solve_ref),
                (land_hbm, land_ref),
                (target_hbm, target_ref),
                (w_in_hbm, w_in_ref),
                (bias_in_hbm, bias_in_ref),
                (land_weight_hbm, land_weight_ref),
                (w_out_hbm, w_out_ref),
                (bias_out_hbm, bias_out_ref),
            )
        )
    ]
    for load in loads:
        load.start()

    barrier = pltpu.get_barrier_semaphore()

    def greet(device):
        pl.semaphore_signal(barrier, inc=1, device_id=device, device_id_type=MESH)

    def greet_member(e):
        greet((e, slab))
        greet((e, other))

    for_peers(slabs, slab, lambda d: greet((ens, d)))
    for_peers(members, ens, greet_member)

    def put(k, src, dst, device, arrived=None):
        pltpu.make_async_remote_copy(
            src_ref=src,
            dst_ref=dst,
            send_sem=send_sem.at[k],
            recv_sem=recv_sem.at[k] if arrived is None else arrived,
            device_id=device,
            device_id_type=MESH,
        ).start()

    mult = lax.rem(code_ref[0], 251) + 2
    base = lax.rem(slab * (lats * lons), PRIME)
    field[0:8, :] = jnp.zeros((8, lons), jnp.float32)
    field[8 + lats : 16 + lats, :] = jnp.zeros((8, lons), jnp.float32)
    loads[0].wait()
    for start in range(0, lats, 8):
        field[8 + start : 16 + start, :] = state_in[start : start + 8, :] + noise(
            mult, base, start, 8, lons
        )
    loads[1].wait()
    prepare_north(coef_ref, north)

    def emit_send(start, count, value):
        for j in range(blocks):
            send[pl.ds(start * blocks + j, count, stride=blocks), :] = value[
                :, j * LANES : (j + 1) * LANES
            ]

    diffuse(field, coef_ref, north, emit_send)

    def chunk_of(step):
        return lax.rem(ens // 2 + 1 + step, chunks)

    def some_rows(device, step):
        return pl.ds(device * blocks + chunk_of(step) * wide, wide)

    pl.semaphore_wait(barrier, slabs - 1 + 2 * (members - 1))
    for step in range(chunks):
        for_peers(
            slabs,
            slab,
            lambda d: put(
                0,
                send.at[some_rows(d, step)],
                recv.at[some_rows(slab, step)],
                (ens, d),
                chunk_sem.at[step],
            ),
        )
    recv[rows_of(slab, blocks), :] = send[rows_of(slab, blocks), :]

    for load in loads[2:]:
        load.wait()
    row = lax.broadcasted_iota(jnp.int32, (levels, levels), 0)
    col = lax.broadcasted_iota(jnp.int32, (levels, levels), 1)
    row_block = jnp.zeros((levels, levels), jnp.int32)
    col_block = jnp.zeros((levels, levels), jnp.int32)
    for j in range(1, bounds_ref.shape[0] - 1):
        row_block += (row >= bounds_ref[j]).astype(jnp.int32)
        col_block += (col >= bounds_ref[j]).astype(jnp.int32)
    solve_s[...] = jnp.where(row_block == col_block, solve_ref[...], 0.0)
    bias = parts_of(bias_in_ref[...] * 0.5)
    land_w = parts_of(land_weight_ref[...] * 0.5)
    land = land_ref[...].astype(jnp.float32)
    extra_row = lax.broadcasted_iota(jnp.int32, (extra, hidden), 0)
    tail = jnp.zeros((extra, hidden), jnp.float32)
    for k, part in enumerate(bias + land_w):
        tail = jnp.where(extra_row == k, part, tail)
    whole = jnp.concatenate([w_in_ref[...].astype(jnp.float32) * 0.5, tail], axis=0)
    w_aug[...] = whole.T.astype(jnp.bfloat16)
    spread = jnp.concatenate(
        [w_out_ref[...].astype(jnp.float32) * 0.5, jnp.zeros((extra, hidden), jnp.float32)], axis=0
    )
    w_back[...] = spread.T.astype(jnp.bfloat16)
    lon_row = lax.broadcasted_iota(jnp.int32, (extra, lons), 0)
    ones = jnp.where(lon_row < 3, 1.0, jnp.where(lon_row < 6, land, 0.0)).astype(jnp.bfloat16)
    bias_col = jnp.sum(jnp.where(row == col, bias_out_ref[...], 0.0), axis=1, keepdims=True)
    for c in range(chunks):
        here = slice(c * width, (c + 1) * width)
        x_aug[c, levels:, :] = ones[:, here]
        shift[c] = bias_col - target_ref[:, here].astype(jnp.float32)
    dy_s[levels:, :] = jnp.zeros((extra, width), jnp.bfloat16)
    grads[...] = jnp.zeros(grads.shape, jnp.float32)

    def column_chunk(step, carry):
        c = chunk_of(step)
        wait_bytes(recv.at[pl.ds(0, (slabs - 1) * wide)], chunk_sem.at[step])
        h = jnp.concatenate(
            [recv[pl.ds(c * wide + j, levels, stride=blocks), :] for j in range(wide)], axis=1
        )
        x = contract(solve_s[...], h, ((1,), (0,)), precision=highest).astype(jnp.bfloat16)
        x_aug[c, 0:levels, :] = x
        x_all = x_aug[c]
        for k in range(0, hidden, hb):
            pre = contract(w_aug[k : k + hb, :], x_all, ((1,), (0,)))
            t = jnp.tanh(pre)
            both = pre * t
            z_s[k : k + hb, :] = (pre + both).astype(jnp.bfloat16)
            slope[k : k + hb, :] = (1.0 + t) * (1.0 + pre - both)
        out = contract(w_out_ref[...], z_s[...], ((1,), (0,)))
        dy = ((out + shift[c]) * (1.0 / members)).astype(jnp.bfloat16)
        dy_s[0:levels, :] = dy
        dy_all = dy_s[...]
        for k in range(0, hidden, hb):
            dz = contract(w_back[k : k + hb, :], dy_all, ((1,), (0,)))
            da_s[k : k + hb, :] = (dz * slope[k : k + hb, :]).astype(jnp.bfloat16)
        dx = contract(w_in_ref[...], da_s[...], ((1,), (0,)))
        dh = contract(solve_s[...], dx, ((0,), (0,)), precision=highest)
        for j in range(wide):
            e = c * wide + j
            back[rows_of(e, levels), :] = dh[:, j * LANES : (j + 1) * LANES]

            @pl.when(e != ens)
            def _():
                put(1, back.at[rows_of(e, levels)], back_in.at[rows_of(ens, levels)], (e, slab))

        for k in range(2):
            part = slice(k * half, (k + 1) * half)
            grads[k, 0:levels, :] += contract(x, da_s[part, :], ((1,), (1,)))
            grads[k, levels:, :] += contract(dy, z_s[part, :], ((1,), (1,)))
        return carry

    lax.fori_loop(0, chunks, column_chunk, 0)

    put(2, grads.at[1 - core], pair_in, (ens, twin))
    back_in[rows_of(ens, levels), :] = back[rows_of(ens, levels), :]
    wait_bytes(pair_in, recv_sem.at[2])
    pair_sum[...] = grads[core] + pair_in[...]

    def plane_device(q):
        return (q // 2, lax.rem(q, 2) * half_slabs + column)

    for_peers(
        planes,
        plane,
        lambda q: put(
            3, pair_sum.at[rows_of(q, rows)], plane_in.at[rows_of(plane, rows)], plane_device(q)
        ),
    )
    plane_in[rows_of(plane, rows), :] = pair_sum[rows_of(plane, rows), :]
    wait_bytes(back_in.at[pl.ds(0, (members - 1) * levels)], recv_sem.at[1])
    summed = back_in[0:levels, :]
    for e in range(1, members):
        summed += back_in[e * levels : (e + 1) * levels, :]
    level_out[...] = summed
    for_peers(
        slabs,
        slab,
        lambda d: put(4, level_out.at[pl.ds(d, 1)], level_in.at[pl.ds(slab, 1)], (ens, d)),
    )
    level_in[pl.ds(slab, 1), :] = level_out[pl.ds(slab, 1), :]
    wait_bytes(plane_in.at[pl.ds(0, (planes - 1) * rows)], recv_sem.at[3])
    summed = plane_in[0:rows, :]
    for q in range(1, planes):
        summed += plane_in[q * rows : (q + 1) * rows, :]

    def height_device(h):
        return (ens, upper * half_slabs + 2 * h + core)

    spot, group = lax.rem(height, near), height // near
    near_in[rows_of(spot, rows), :] = summed
    mine = rows_of(spot, rows)
    for k in range(1, near):
        peer = group * near + lax.rem(spot + k, near)
        put(5, near_in.at[mine], near_in.at[mine], height_device(peer))
    wait_bytes(near_in.at[pl.ds(0, (near - 1) * rows)], recv_sem.at[5])
    summed = near_in[0:rows, :]
    for k in range(1, near):
        summed += near_in[k * rows : (k + 1) * rows, :]
    from_far = rows_of(group, rows)
    far_in[from_far, :] = summed
    for k in range(1, far):
        peer = lax.rem(height + k * near, heights)
        put(6, far_in.at[from_far], far_in.at[from_far], height_device(peer))
    wait_bytes(level_in.at[pl.ds(0, slabs - 1)], recv_sem.at[4])
    for_peers(
        members, ens, lambda e: put(7, level_in, field_in.at[rows_of(ens, lats)], (e, slab))
    )
    field_in[rows_of(ens, lats), :] = level_in[...]
    wait_bytes(far_in.at[pl.ds(0, (far - 1) * rows)], recv_sem.at[6])
    summed = far_in[0:rows, :]
    for k in range(1, far):
        summed += far_in[k * rows : (k + 1) * rows, :]
    piece[...] = summed
    for_peers(
        planes,
        plane,
        lambda q: put(8, piece, half_all.at[rows_of(plane, rows)], plane_device(q)),
    )
    half_all[rows_of(plane, rows), :] = piece[...]
    wait_bytes(field_in.at[pl.ds(0, (members - 1) * lats)], recv_sem.at[7])
    for e in range(members):
        field[8 : 8 + lats, e * LANES : (e + 1) * LANES] = field_in[e * lats : (e + 1) * lats, :]

    def emit_state(start, count, value):
        state_ref[start : start + count, :] = value

    diffuse(field, coef_ref, north, emit_state)
    wait_bytes(half_all.at[pl.ds(0, (planes - 1) * rows)], recv_sem.at[8])
    put(9, half_all, twin_all, (ens, twin))
    total_ref[core] = half_all[...]
    wait_bytes(send.at[pl.ds(0, (slabs - 1) * blocks)], send_sem.at[0])
    wait_bytes(back.at[pl.ds(0, (members - 1) * levels)], send_sem.at[1])
    wait_bytes(pair_in, send_sem.at[2])
    wait_bytes(plane_in.at[pl.ds(0, (planes - 1) * rows)], send_sem.at[3])
    wait_bytes(level_in.at[pl.ds(0, slabs - 1)], send_sem.at[4])
    wait_bytes(near_in.at[pl.ds(0, (near - 1) * rows)], send_sem.at[5])
    wait_bytes(far_in.at[pl.ds(0, (far - 1) * rows)], send_sem.at[6])
    wait_bytes(field_in.at[pl.ds(0, (members - 1) * lats)], send_sem.at[7])
    wait_bytes(half_all.at[pl.ds(0, (planes - 1) * rows)], send_sem.at[8])
    wait_bytes(twin_all, recv_sem.at[9])
    total_ref[1 - core] = twin_all[...]
    wait_bytes(twin_all, send_sem.at[9])


def finish_kernel(total_ref, grad_ref, in_ref, out_ref, state_ref):
    levels, hidden = in_ref.shape
    half = hidden // 2
    for ref, first in ((in_ref, 0), (out_ref, levels)):
        square = jnp.zeros((1, 1), jnp.float32)
        for k in range(2):
            grad = total_ref[k, first : first + levels, :]
            square += jnp.sum(jnp.sum(grad * grad, axis=0, keepdims=True), axis=1, keepdims=True)
        scale = 1.0 / jnp.sqrt(square * (1.0 / (levels * hidden)) + 1e-06)
        for k in range(2):
            ref[:, k * half : (k + 1) * half] = total_ref[k, first : first + levels, :] * scale
    state_ref[...] = grad_ref[...]


def on_device(
    members,
    slabs,
    state,
    face_coefs,
    codes,
    acoustic_inv,
    bounds,
    land_mask,
    target,
    w_in,
    bias_in,
    land_weight,
    w_out,
    bias_out,
):
    _, lats, lons = state.shape
    levels, hidden = w_in.shape
    blocks = lons // LANES
    f32, bf16 = jnp.float32, jnp.bfloat16
    vmem = pl.BlockSpec(memory_space=pltpu.VMEM)
    smem = pl.BlockSpec(memory_space=pltpu.SMEM)
    hbm = pl.BlockSpec(memory_space=pltpu.HBM)
    like = jax.ShapeDtypeStruct
    dma = pltpu.SemaphoreType.DMA
    pad = 2 * levels if levels >= 64 else levels + 16
    width = 2 * LANES
    chunks = lons // width
    half = hidden // 2
    planes = 2 * members
    rows = 2 * levels // planes
    heights = slabs // 4
    near = 4 if heights >= 16 else 2
    far = heights // near
    fetched = (
        state.reshape(lats, lons),
        face_coefs.reshape(2, lats, lons),
        acoustic_inv.reshape(levels, levels),
        land_mask,
        target.reshape(levels, lons),
        w_in,
        bias_in.reshape(1, hidden),
        land_weight.reshape(1, hidden),
        w_out.T,
        bias_out.reshape(1, levels),
    )
    grad_state, total = pl.pallas_call(
        functools.partial(step_kernel, members, slabs),
        out_shape=(like((lats, lons), f32), like((2, 2 * levels, half), f32)),
        in_specs=[hbm] * len(fetched) + [smem, smem],
        out_specs=(vmem, vmem),
        scratch_shapes=[pltpu.VMEM(v.shape, v.dtype) for v in fetched]
        + [
            pltpu.VMEM((lats + 16, lons), f32),
            pltpu.VMEM((lats + 8, lons), f32),
            pltpu.VMEM((lats * blocks, LANES), f32),
            pltpu.VMEM((levels * blocks, LANES), f32),
            pltpu.VMEM((levels, levels), f32),
            pltpu.VMEM((hidden, pad), bf16),
            pltpu.VMEM((hidden, pad), bf16),
            pltpu.VMEM((chunks, pad, width), bf16),
            pltpu.VMEM((chunks, levels, width), f32),
            pltpu.VMEM((hidden, width), bf16),
            pltpu.VMEM((hidden, width), f32),
            pltpu.VMEM((pad, width), bf16),
            pltpu.VMEM((hidden, width), bf16),
            pltpu.VMEM((members * levels, LANES), f32),
            pltpu.VMEM((members * levels, LANES), f32),
            pltpu.VMEM((2, 2 * levels, half), f32),
            pltpu.VMEM((2 * levels, half), f32),
            pltpu.VMEM((2 * levels, half), f32),
            pltpu.VMEM((planes * rows, half), f32),
            pltpu.VMEM((near * rows, half), f32),
            pltpu.VMEM((far * rows, half), f32),
            pltpu.VMEM((rows, half), f32),
            pltpu.VMEM((levels, LANES), f32),
            pltpu.VMEM((lats, LANES), f32),
            pltpu.VMEM((members * lats, LANES), f32),
            pltpu.VMEM((2 * levels, half), f32),
            pltpu.VMEM((2 * levels, half), f32),
            dma((len(fetched),)),
            dma((chunks,)),
            dma((10,)),
            dma((10,)),
        ],
        compiler_params=pltpu.CompilerParams(
            collective_id=0, has_side_effects=True, vmem_limit_bytes=40 * 1024 * 1024
        ),
    )(*fetched, codes, bounds)
    upd_in, upd_out, grad_state = pl.pallas_call(
        finish_kernel,
        out_shape=(
            like((levels, hidden), f32),
            like((levels, hidden), f32),
            like((lats, lons), f32),
        ),
        in_specs=[vmem] * 2,
        out_specs=(vmem,) * 3,
        compiler_params=pltpu.CompilerParams(vmem_limit_bytes=16 * 1024 * 1024),
    )(total, grad_state)
    return upd_in, upd_out.T, grad_state.reshape(state.shape)


def solution(mesh):
    placed = (
        P("slab", None, None),
        P(None, "slab", None, None),
        P("ens"),
        P("slab", None, None),
        P(),
        P("slab", None),
        P(None, "slab", None),
        P(),
        P(),
        P(),
        P(),
        P(),
    )
    return jax.shard_map(
        functools.partial(on_device, mesh.shape["ens"], mesh.shape["slab"]),
        mesh=mesh,
        in_specs=placed,
        out_specs=(P(), P(), P("slab", None, None)),
        check_vma=False,
    )
```

```python
import functools

import jax
import jax.numpy as jnp
from jax import lax
from jax.experimental import pallas as pl
from jax.experimental.pallas import tpu as pltpu
from jax.sharding import PartitionSpec as P

MESH = pl.DeviceIdType.MESH
LANES = 128
PRIME = 65521


def reduced(value):
    value = (value & 65535) + 15 * (value >> 16)
    return value


def below_prime(value):
    return jnp.where(value >= PRIME, value - PRIME, value)


def noise(mult, base, first_row, rows, lons):
    shape = (rows, lons)
    row = lax.broadcasted_iota(jnp.int32, shape, 0) + first_row
    cell = below_prime(row * lons + lax.broadcasted_iota(jnp.int32, shape, 1) + base)
    first = below_prime(reduced(mult * cell + 12345))
    second = below_prime(reduced(reduced(first * 31337 + mult)))
    return second.astype(jnp.float32) * (1.0 / PRIME) - 0.5


def prepare_north(coef_ref, north):
    lats, lons = coef_ref.shape[1:]
    north[0:8, :] = jnp.zeros((8, lons), jnp.float32)
    for start in range(0, lats, 16):
        part = coef_ref[1, start : start + 16, :].astype(jnp.float32)
        if start + 16 >= lats:
            row = lax.broadcasted_iota(jnp.int32, part.shape, 0) + start
            part = jnp.where(row < lats - 1, part, 0.0)
        north[8 + start : 8 + start + part.shape[0], :] = part


def diffuse(field, coef_ref, north, emit):
    lats, lons = coef_ref.shape[1:]
    step = min(16, lats)
    for start in range(0, lats, step):
        here = field[8 + start : 8 + start + step, :]
        ahead = field[9 + start : 9 + start + step, :]
        behind = field[7 + start : 7 + start + step, :]
        east = coef_ref[0, start : start + step, :].astype(jnp.float32)
        flux_x = east * (pltpu.roll(here, lons - 1, 1) - here)
        flux_y = north[8 + start : 8 + start + step, :] * (ahead - here)
        lower = north[7 + start : 7 + start + step, :] * (here - behind)
        emit(start, step, here + flux_x - pltpu.roll(flux_x, 1, 1) + flux_y - lower)


def offset_of(step, count):
    step = count - 2 - step
    half = step // 2 + 1
    return jnp.where(step % 2 == 0, half, count - half)


def for_peers(count, me, body):
    def one(step, carry):
        body(lax.rem(me + offset_of(step, count), count))
        return carry

    lax.fori_loop(0, count - 1, one, 0)


def wait_bytes(ref, sem):
    pltpu.make_async_copy(ref, ref, sem).wait()


def rows_of(index, size):
    return pl.ds(pl.multiple_of(index * size, size), size)


def parts_of(value):
    high = value.astype(jnp.bfloat16).astype(jnp.float32)
    rest = value - high
    middle = rest.astype(jnp.bfloat16).astype(jnp.float32)
    return high, middle, rest - middle


def contract(a, b, dims, **kw):
    return lax.dot_general(a, b, (dims, ((), ())), preferred_element_type=jnp.float32, **kw)


def step_kernel(
    members,
    slabs,
    state_hbm,
    coef_hbm,
    solve_hbm,
    land_hbm,
    target_hbm,
    w_in_hbm,
    bias_in_hbm,
    land_weight_hbm,
    w_out_hbm,
    bias_out_hbm,
    code_ref,
    bounds_ref,
    state_hbm_out,
    total_hbm,
    state_in,
    coef_ref,
    solve_ref,
    land_ref,
    target_ref,
    w_in_ref,
    bias_in_ref,
    land_weight_ref,
    w_out_ref,
    bias_out_ref,
    field,
    north,
    send,
    recv,
    solve_s,
    w_aug,
    w_back,
    x_aug,
    shift,
    z_s,
    slope,
    dy_s,
    da_s,
    back,
    back_in,
    grads,
    pair_in,
    pair_sum,
    plane_in,
    near_in,
    far_in,
    piece,
    level_out,
    level_in,
    field_in,
    half_all,
    load_sem,
    store_sem,
    chunk_sem,
    plane_sem,
    send_sem,
    recv_sem,
):
    ens, slab = lax.axis_index("ens"), lax.axis_index("slab")
    lats, lons = state_in.shape
    levels, hidden = w_in_ref.shape
    blocks = lons // LANES
    chunks, pad, width = x_aug.shape
    wide = width // LANES
    extra = pad - levels
    hb = min(128, hidden)
    core = lax.rem(slab, 2)
    twin = slab + 1 - 2 * core
    half_slabs = slabs // 2
    upper = slab // half_slabs
    other = lax.rem(slab + half_slabs, slabs)
    column = lax.rem(slab, half_slabs)
    near = near_in.shape[0] // piece.shape[0]
    far = far_in.shape[0] // piece.shape[0]
    heights = near * far
    height = column // 2
    plane = ens * 2 + upper
    planes = members * 2
    rows = piece.shape[0]
    half = hidden // 2
    highest = lax.Precision.HIGHEST

    loads = [
        pltpu.make_async_copy(src, dst, load_sem.at[k])
        for k, (src, dst) in enumerate(
            (
                (state_hbm, state_in),
                (coef_hbm, coef_ref),
                (solve_hbm, solve_ref),
                (land_hbm, land_ref),
                (target_hbm, target_ref),
                (w_in_hbm, w_in_ref),
                (bias_in_hbm, bias_in_ref),
                (land_weight_hbm, land_weight_ref),
                (w_out_hbm, w_out_ref),
                (bias_out_hbm, bias_out_ref),
            )
        )
    ]
    for load in loads:
        load.start()

    barrier = pltpu.get_barrier_semaphore()

    def greet(device):
        pl.semaphore_signal(barrier, inc=1, device_id=device, device_id_type=MESH)

    def greet_member(e):
        greet((e, slab))
        greet((e, other))

    for_peers(slabs, slab, lambda d: greet((ens, d)))
    for_peers(members, ens, greet_member)

    def put(k, src, dst, device, arrived=None):
        pltpu.make_async_remote_copy(
            src_ref=src,
            dst_ref=dst,
            send_sem=send_sem.at[k],
            recv_sem=recv_sem.at[k] if arrived is None else arrived,
            device_id=device,
            device_id_type=MESH,
        ).start()

    mult = lax.rem(code_ref[0], 251) + 2
    base = lax.rem(slab * (lats * lons), PRIME)
    field[0:8, :] = jnp.zeros((8, lons), jnp.float32)
    field[8 + lats : 16 + lats, :] = jnp.zeros((8, lons), jnp.float32)
    loads[0].wait()
    for start in range(0, lats, 8):
        field[8 + start : 16 + start, :] = state_in[start : start + 8, :] + noise(
            mult, base, start, 8, lons
        )
    loads[1].wait()
    prepare_north(coef_ref, north)

    def emit_send(start, count, value):
        for j in range(blocks):
            send[pl.ds(start * blocks + j, count, stride=blocks), :] = value[
                :, j * LANES : (j + 1) * LANES
            ]

    diffuse(field, coef_ref, north, emit_send)

    def chunk_of(step):
        return lax.rem(ens // 2 + 1 + step, chunks)

    def some_rows(device, step):
        return pl.ds(device * blocks + chunk_of(step) * wide, wide)

    pl.semaphore_wait(barrier, slabs - 1 + 2 * (members - 1))
    for step in range(chunks):
        for_peers(
            slabs,
            slab,
            lambda d: put(
                0,
                send.at[some_rows(d, step)],
                recv.at[some_rows(slab, step)],
                (ens, d),
                chunk_sem.at[step],
            ),
        )
    recv[rows_of(slab, blocks), :] = send[rows_of(slab, blocks), :]

    for load in loads[2:]:
        load.wait()
    row = lax.broadcasted_iota(jnp.int32, (levels, levels), 0)
    col = lax.broadcasted_iota(jnp.int32, (levels, levels), 1)
    row_block = jnp.zeros((levels, levels), jnp.int32)
    col_block = jnp.zeros((levels, levels), jnp.int32)
    for j in range(1, bounds_ref.shape[0] - 1):
        row_block += (row >= bounds_ref[j]).astype(jnp.int32)
        col_block += (col >= bounds_ref[j]).astype(jnp.int32)
    solve_s[...] = jnp.where(row_block == col_block, solve_ref[...], 0.0)
    bias = parts_of(bias_in_ref[...] * 0.5)
    land_w = parts_of(land_weight_ref[...] * 0.5)
    land = land_ref[...].astype(jnp.float32)
    extra_row = lax.broadcasted_iota(jnp.int32, (extra, hidden), 0)
    tail = jnp.zeros((extra, hidden), jnp.float32)
    for k, part in enumerate(bias + land_w):
        tail = jnp.where(extra_row == k, part, tail)
    whole = jnp.concatenate([w_in_ref[...].astype(jnp.float32) * 0.5, tail], axis=0)
    w_aug[...] = whole.T.astype(jnp.bfloat16)
    spread = jnp.concatenate(
        [w_out_ref[...].astype(jnp.float32) * 0.5, jnp.zeros((extra, hidden), jnp.float32)], axis=0
    )
    w_back[...] = spread.T.astype(jnp.bfloat16)
    lon_row = lax.broadcasted_iota(jnp.int32, (extra, lons), 0)
    ones = jnp.where(lon_row < 3, 1.0, jnp.where(lon_row < 6, land, 0.0)).astype(jnp.bfloat16)
    bias_col = jnp.sum(jnp.where(row == col, bias_out_ref[...], 0.0), axis=1, keepdims=True)
    for c in range(chunks):
        here = slice(c * width, (c + 1) * width)
        x_aug[c, levels:, :] = ones[:, here]
        shift[c] = bias_col - target_ref[:, here].astype(jnp.float32)
    dy_s[levels:, :] = jnp.zeros((extra, width), jnp.bfloat16)
    grads[...] = jnp.zeros(grads.shape, jnp.float32)

    def gradient(k, x, dy):
        part = rows_of(k, half)
        grads[k, 0:levels, :] += contract(x, da_s[part, :], ((1,), (1,)))
        grads[k, levels:, :] += contract(dy, z_s[part, :], ((1,), (1,)))

    def to_member(e):
        put(1, back.at[rows_of(e, levels)], back_in.at[rows_of(ens, levels)], (e, slab))

    def column_chunk(step, last):
        c = chunk_of(step)
        wait_bytes(recv.at[pl.ds(0, (slabs - 1) * wide)], chunk_sem.at[step])
        h = jnp.concatenate(
            [recv[pl.ds(c * wide + j, levels, stride=blocks), :] for j in range(wide)], axis=1
        )
        x = contract(solve_s[...], h, ((1,), (0,)), precision=highest).astype(jnp.bfloat16)
        x_aug[c, 0:levels, :] = x
        x_all = x_aug[c]
        for k in range(0, hidden, hb):
            pre = contract(w_aug[k : k + hb, :], x_all, ((1,), (0,)))
            t = jnp.tanh(pre)
            both = pre * t
            z_s[k : k + hb, :] = (pre + both).astype(jnp.bfloat16)
            slope[k : k + hb, :] = (1.0 + t) * (1.0 + pre - both)
        out = contract(w_out_ref[...], z_s[...], ((1,), (0,)))
        dy = ((out + shift[c]) * (1.0 / members)).astype(jnp.bfloat16)
        dy_s[0:levels, :] = dy
        dy_all = dy_s[...]
        for k in range(0, hidden, hb):
            dz = contract(w_back[k : k + hb, :], dy_all, ((1,), (0,)))
            da_s[k : k + hb, :] = (dz * slope[k : k + hb, :]).astype(jnp.bfloat16)
        if last:
            gradient(1 - core, x, dy)
            put(2, grads.at[1 - core], pair_in, (ens, twin))
        dx = contract(w_in_ref[...], da_s[...], ((1,), (0,)))
        dh = contract(solve_s[...], dx, ((0,), (0,)), precision=highest)
        for j in range(wide):
            e = c * wide + j
            back[rows_of(e, levels), :] = dh[:, j * LANES : (j + 1) * LANES]
            pl.when(e != ens)(functools.partial(to_member, e))
        if last:
            gradient(core, x, dy)
        else:
            gradient(0, x, dy)
            gradient(1, x, dy)

    def column_step(step, carry):
        column_chunk(step, False)
        return carry

    lax.fori_loop(0, chunks - 1, column_step, 0)
    column_chunk(chunks - 1, True)
    back_in[rows_of(ens, levels), :] = back[rows_of(ens, levels), :]
    wait_bytes(pair_in, recv_sem.at[2])
    pair_sum[...] = grads[core] + pair_in[...]

    def plane_device(q):
        return (q // 2, lax.rem(q, 2) * half_slabs + column)

    for_peers(
        planes,
        plane,
        lambda q: put(
            3, pair_sum.at[rows_of(q, rows)], plane_in.at[rows_of(plane, rows)], plane_device(q)
        ),
    )
    plane_in[rows_of(plane, rows), :] = pair_sum[rows_of(plane, rows), :]
    wait_bytes(back_in.at[pl.ds(0, (members - 1) * levels)], recv_sem.at[1])
    summed = back_in[0:levels, :]
    for e in range(1, members):
        summed += back_in[e * levels : (e + 1) * levels, :]
    level_out[...] = summed
    for_peers(
        slabs,
        slab,
        lambda d: put(4, level_out.at[pl.ds(d, 1)], level_in.at[pl.ds(slab, 1)], (ens, d)),
    )
    level_in[pl.ds(slab, 1), :] = level_out[pl.ds(slab, 1), :]
    wait_bytes(plane_in.at[pl.ds(0, (planes - 1) * rows)], recv_sem.at[3])
    summed = plane_in[0:rows, :]
    for q in range(1, planes):
        summed += plane_in[q * rows : (q + 1) * rows, :]

    def height_device(h):
        return (ens, upper * half_slabs + 2 * h + core)

    spot, group = lax.rem(height, near), height // near
    near_in[rows_of(spot, rows), :] = summed
    mine = rows_of(spot, rows)
    for k in range(1, near):
        peer = group * near + lax.rem(spot + k, near)
        put(5, near_in.at[mine], near_in.at[mine], height_device(peer))
    wait_bytes(near_in.at[pl.ds(0, (near - 1) * rows)], recv_sem.at[5])
    summed = near_in[0:rows, :]
    for k in range(1, near):
        summed += near_in[k * rows : (k + 1) * rows, :]
    from_far = rows_of(group, rows)
    far_in[from_far, :] = summed
    for k in range(1, far):
        peer = lax.rem(height + k * near, heights)
        put(6, far_in.at[from_far], far_in.at[from_far], height_device(peer))
    wait_bytes(level_in.at[pl.ds(0, slabs - 1)], recv_sem.at[4])
    for_peers(
        members, ens, lambda e: put(7, level_in, field_in.at[rows_of(ens, lats)], (e, slab))
    )
    field_in[rows_of(ens, lats), :] = level_in[...]
    wait_bytes(far_in.at[pl.ds(0, (far - 1) * rows)], recv_sem.at[6])
    summed = far_in[0:rows, :]
    for k in range(1, far):
        summed += far_in[k * rows : (k + 1) * rows, :]
    piece[...] = summed
    for_peers(
        planes,
        plane,
        lambda q: put(
            8, piece, half_all.at[rows_of(plane, rows)], plane_device(q), plane_sem.at[plane]
        ),
    )
    half_all[rows_of(plane, rows), :] = piece[...]

    def to_twin(q):
        at = rows_of(q, rows)
        put(9, half_all.at[at], total_hbm.at[core, at], (ens, twin))

    to_twin(plane)
    wait_bytes(field_in.at[pl.ds(0, (members - 1) * lats)], recv_sem.at[7])
    for e in range(members):
        field[8 : 8 + lats, e * LANES : (e + 1) * LANES] = field_in[e * lats : (e + 1) * lats, :]

    def emit_state(start, count, value):
        state_in[start : start + count, :] = value

    diffuse(field, coef_ref, north, emit_state)
    store_state = pltpu.make_async_copy(state_in, state_hbm_out, store_sem.at[0])
    store_state.start()

    def forward(q):
        wait_bytes(half_all.at[rows_of(q, rows)], plane_sem.at[q])
        to_twin(q)

    for_peers(planes, plane, forward)
    store_half = pltpu.make_async_copy(half_all, total_hbm.at[core], store_sem.at[1])
    store_half.start()
    wait_bytes(send.at[pl.ds(0, (slabs - 1) * blocks)], send_sem.at[0])
    wait_bytes(back.at[pl.ds(0, (members - 1) * levels)], send_sem.at[1])
    wait_bytes(pair_in, send_sem.at[2])
    wait_bytes(plane_in.at[pl.ds(0, (planes - 1) * rows)], send_sem.at[3])
    wait_bytes(level_in.at[pl.ds(0, slabs - 1)], send_sem.at[4])
    wait_bytes(near_in.at[pl.ds(0, (near - 1) * rows)], send_sem.at[5])
    wait_bytes(far_in.at[pl.ds(0, (far - 1) * rows)], send_sem.at[6])
    wait_bytes(field_in.at[pl.ds(0, (members - 1) * lats)], send_sem.at[7])
    wait_bytes(half_all.at[pl.ds(0, (planes - 1) * rows)], send_sem.at[8])
    wait_bytes(half_all, send_sem.at[9])
    store_state.wait()
    store_half.wait()
    wait_bytes(total_hbm.at[1 - core], recv_sem.at[9])


def finish_kernel(total_ref, grad_ref, in_ref, out_ref, state_ref):
    levels, hidden = in_ref.shape
    half = hidden // 2
    for ref, first in ((in_ref, 0), (out_ref, levels)):
        square = jnp.zeros((1, 1), jnp.float32)
        for k in range(2):
            grad = total_ref[k, first : first + levels, :]
            square += jnp.sum(jnp.sum(grad * grad, axis=0, keepdims=True), axis=1, keepdims=True)
        scale = 1.0 / jnp.sqrt(square * (1.0 / (levels * hidden)) + 1e-06)
        for k in range(2):
            ref[:, k * half : (k + 1) * half] = total_ref[k, first : first + levels, :] * scale
    state_ref[...] = grad_ref[...]


def on_device(
    members,
    slabs,
    state,
    face_coefs,
    codes,
    acoustic_inv,
    bounds,
    land_mask,
    target,
    w_in,
    bias_in,
    land_weight,
    w_out,
    bias_out,
):
    _, lats, lons = state.shape
    levels, hidden = w_in.shape
    blocks = lons // LANES
    f32, bf16 = jnp.float32, jnp.bfloat16
    vmem = pl.BlockSpec(memory_space=pltpu.VMEM)
    smem = pl.BlockSpec(memory_space=pltpu.SMEM)
    hbm = pl.BlockSpec(memory_space=pltpu.HBM)
    like = jax.ShapeDtypeStruct
    dma = pltpu.SemaphoreType.DMA
    pad = 2 * levels if levels >= 64 else levels + 16
    width = 2 * LANES
    chunks = lons // width
    half = hidden // 2
    planes = 2 * members
    rows = 2 * levels // planes
    heights = slabs // 4
    near = 4 if heights >= 16 else 2
    far = heights // near
    fetched = (
        state.reshape(lats, lons),
        face_coefs.reshape(2, lats, lons),
        acoustic_inv.reshape(levels, levels),
        land_mask,
        target.reshape(levels, lons),
        w_in,
        bias_in.reshape(1, hidden),
        land_weight.reshape(1, hidden),
        w_out.T,
        bias_out.reshape(1, levels),
    )
    grad_state, total = pl.pallas_call(
        functools.partial(step_kernel, members, slabs),
        out_shape=(like((lats, lons), f32), like((2, 2 * levels, half), f32)),
        in_specs=[hbm] * len(fetched) + [smem, smem],
        out_specs=(hbm, hbm),
        scratch_shapes=[pltpu.VMEM(v.shape, v.dtype) for v in fetched]
        + [
            pltpu.VMEM((lats + 16, lons), f32),
            pltpu.VMEM((lats + 8, lons), f32),
            pltpu.VMEM((lats * blocks, LANES), f32),
            pltpu.VMEM((levels * blocks, LANES), f32),
            pltpu.VMEM((levels, levels), f32),
            pltpu.VMEM((hidden, pad), bf16),
            pltpu.VMEM((hidden, pad), bf16),
            pltpu.VMEM((chunks, pad, width), bf16),
            pltpu.VMEM((chunks, levels, width), f32),
            pltpu.VMEM((hidden, width), bf16),
            pltpu.VMEM((hidden, width), f32),
            pltpu.VMEM((pad, width), bf16),
            pltpu.VMEM((hidden, width), bf16),
            pltpu.VMEM((members * levels, LANES), f32),
            pltpu.VMEM((members * levels, LANES), f32),
            pltpu.VMEM((2, 2 * levels, half), f32),
            pltpu.VMEM((2 * levels, half), f32),
            pltpu.VMEM((2 * levels, half), f32),
            pltpu.VMEM((planes * rows, half), f32),
            pltpu.VMEM((near * rows, half), f32),
            pltpu.VMEM((far * rows, half), f32),
            pltpu.VMEM((rows, half), f32),
            pltpu.VMEM((levels, LANES), f32),
            pltpu.VMEM((lats, LANES), f32),
            pltpu.VMEM((members * lats, LANES), f32),
            pltpu.VMEM((2 * levels, half), f32),
            dma((len(fetched),)),
            dma((2,)),
            dma((chunks,)),
            dma((planes,)),
            dma((10,)),
            dma((10,)),
        ],
        compiler_params=pltpu.CompilerParams(
            collective_id=0, has_side_effects=True, vmem_limit_bytes=56 * 1024 * 1024
        ),
    )(*fetched, codes, bounds)
    upd_in, upd_out, grad_state = pl.pallas_call(
        finish_kernel,
        out_shape=(
            like((levels, hidden), f32),
            like((levels, hidden), f32),
            like((lats, lons), f32),
        ),
        in_specs=[vmem] * 2,
        out_specs=(vmem,) * 3,
        compiler_params=pltpu.CompilerParams(vmem_limit_bytes=56 * 1024 * 1024),
    )(total, grad_state)
    return upd_in, upd_out.T, grad_state.reshape(state.shape)


def solution(mesh):
    placed = (
        P("slab", None, None),
        P(None, "slab", None, None),
        P("ens"),
        P("slab", None, None),
        P(),
        P("slab", None),
        P(None, "slab", None),
        P(),
        P(),
        P(),
        P(),
        P(),
    )
    return jax.shard_map(
        functools.partial(on_device, mesh.shape["ens"], mesh.shape["slab"]),
        mesh=mesh,
        in_specs=placed,
        out_specs=(P(), P(), P("slab", None, None)),
        check_vma=False,
    )
```

```python
import functools

import jax
import jax.numpy as jnp
from jax import lax
from jax.experimental import pallas as pl
from jax.experimental.pallas import tpu as pltpu
from jax.sharding import PartitionSpec as P

MESH = pl.DeviceIdType.MESH
LANES = 128
PRIME = 65521


def reduced(value):
    value = (value & 65535) + 15 * (value >> 16)
    return value


def below_prime(value):
    return jnp.where(value >= PRIME, value - PRIME, value)


def noise(mult, base, first_row, rows, lons):
    shape = (rows, lons)
    row = lax.broadcasted_iota(jnp.int32, shape, 0) + first_row
    cell = below_prime(row * lons + lax.broadcasted_iota(jnp.int32, shape, 1) + base)
    first = below_prime(reduced(mult * cell + 12345))
    second = below_prime(reduced(reduced(first * 31337 + mult)))
    return second.astype(jnp.float32) * (1.0 / PRIME) - 0.5


def prepare_north(coef_ref, north):
    lats, lons = coef_ref.shape[1:]
    north[0:8, :] = jnp.zeros((8, lons), jnp.float32)
    for start in range(0, lats, 16):
        part = coef_ref[1, start : start + 16, :].astype(jnp.float32)
        if start + 16 >= lats:
            row = lax.broadcasted_iota(jnp.int32, part.shape, 0) + start
            part = jnp.where(row < lats - 1, part, 0.0)
        north[8 + start : 8 + start + part.shape[0], :] = part


def diffuse(field, coef_ref, north, emit):
    lats, lons = coef_ref.shape[1:]
    step = min(16, lats)
    for start in range(0, lats, step):
        here = field[8 + start : 8 + start + step, :]
        ahead = field[9 + start : 9 + start + step, :]
        behind = field[7 + start : 7 + start + step, :]
        east = coef_ref[0, start : start + step, :].astype(jnp.float32)
        flux_x = east * (pltpu.roll(here, lons - 1, 1) - here)
        flux_y = north[8 + start : 8 + start + step, :] * (ahead - here)
        lower = north[7 + start : 7 + start + step, :] * (here - behind)
        emit(start, step, here + flux_x - pltpu.roll(flux_x, 1, 1) + flux_y - lower)


def for_peers(count, me, body):
    far = count // 2
    body(lax.rem(me + far, count))

    def both(step, carry):
        body(lax.rem(me + (far - step), count))
        body(lax.rem(me + (far + step), count))
        return carry

    lax.fori_loop(1, far, both, 0)


def wait_bytes(ref, sem):
    pltpu.make_async_copy(ref, ref, sem).wait()


def rows_of(index, size):
    return pl.ds(pl.multiple_of(index * size, size), size)


def parts_of(value):
    high = value.astype(jnp.bfloat16).astype(jnp.float32)
    rest = value - high
    middle = rest.astype(jnp.bfloat16).astype(jnp.float32)
    return high, middle, rest - middle


def contract(a, b, dims, **kw):
    return lax.dot_general(a, b, (dims, ((), ())), preferred_element_type=jnp.float32, **kw)


def step_kernel(
    members,
    slabs,
    state_hbm,
    coef_hbm,
    solve_hbm,
    land_hbm,
    target_hbm,
    w_in_hbm,
    bias_in_hbm,
    land_weight_hbm,
    w_out_hbm,
    bias_out_hbm,
    code_ref,
    bounds_ref,
    state_hbm_out,
    total_hbm,
    state_in,
    coef_ref,
    solve_ref,
    land_ref,
    target_ref,
    w_in_ref,
    bias_in_ref,
    land_weight_ref,
    w_out_ref,
    bias_out_ref,
    field,
    north,
    send,
    recv,
    solve_s,
    w_aug,
    w_back,
    x_aug,
    shift,
    z_s,
    slope,
    dy_s,
    da_s,
    back,
    back_in,
    grads,
    pair_in,
    pair_sum,
    plane_in,
    near_in,
    far_in,
    piece,
    level_out,
    level_in,
    field_in,
    half_all,
    load_sem,
    store_sem,
    chunk_sem,
    plane_sem,
    send_sem,
    recv_sem,
):
    ens, slab = lax.axis_index("ens"), lax.axis_index("slab")
    lats, lons = state_in.shape
    levels, hidden = w_in_ref.shape
    blocks = lons // LANES
    chunks, pad, width = x_aug.shape
    wide = width // LANES
    extra = pad - levels
    hb = min(128, hidden)
    core = lax.rem(slab, 2)
    twin = slab + 1 - 2 * core
    half_slabs = slabs // 2
    upper = slab // half_slabs
    other = lax.rem(slab + half_slabs, slabs)
    column = lax.rem(slab, half_slabs)
    near = near_in.shape[0] // piece.shape[0]
    far = far_in.shape[0] // piece.shape[0]
    heights = near * far
    height = column // 2
    plane = ens * 2 + upper
    planes = members * 2
    rows = piece.shape[0]
    half = hidden // 2
    highest = lax.Precision.HIGHEST

    loads = [
        pltpu.make_async_copy(src, dst, load_sem.at[k])
        for k, (src, dst) in enumerate(
            (
                (state_hbm, state_in),
                (coef_hbm, coef_ref),
                (solve_hbm, solve_ref),
                (land_hbm, land_ref),
                (target_hbm, target_ref),
                (w_in_hbm, w_in_ref),
                (bias_in_hbm, bias_in_ref),
                (land_weight_hbm, land_weight_ref),
                (w_out_hbm, w_out_ref),
                (bias_out_hbm, bias_out_ref),
            )
        )
    ]
    for load in loads:
        load.start()

    barrier = pltpu.get_barrier_semaphore()

    def greet(device):
        pl.semaphore_signal(barrier, inc=1, device_id=device, device_id_type=MESH)

    def greet_member(e):
        greet((e, slab))
        greet((e, other))

    for_peers(slabs, slab, lambda d: greet((ens, d)))
    for_peers(members, ens, greet_member)

    def put(k, src, dst, device, arrived=None):
        pltpu.make_async_remote_copy(
            src_ref=src,
            dst_ref=dst,
            send_sem=send_sem.at[k],
            recv_sem=recv_sem.at[k] if arrived is None else arrived,
            device_id=device,
            device_id_type=MESH,
        ).start()

    mult = lax.rem(code_ref[0], 251) + 2
    base = lax.rem(slab * (lats * lons), PRIME)
    field[0:8, :] = jnp.zeros((8, lons), jnp.float32)
    field[8 + lats : 16 + lats, :] = jnp.zeros((8, lons), jnp.float32)
    loads[0].wait()
    for start in range(0, lats, 8):
        field[8 + start : 16 + start, :] = state_in[start : start + 8, :] + noise(
            mult, base, start, 8, lons
        )
    loads[1].wait()
    prepare_north(coef_ref, north)

    def emit_send(start, count, value):
        for j in range(blocks):
            send[pl.ds(start * blocks + j, count, stride=blocks), :] = value[
                :, j * LANES : (j + 1) * LANES
            ]

    diffuse(field, coef_ref, north, emit_send)

    def chunk_of(step):
        return lax.rem(ens // 2 + 1 + step, chunks)

    def some_rows(device, step):
        return pl.ds(device * blocks + chunk_of(step) * wide, wide)

    pl.semaphore_wait(barrier, slabs - 1 + 2 * (members - 1))
    for step in range(chunks):
        for_peers(
            slabs,
            slab,
            lambda d: put(
                0,
                send.at[some_rows(d, step)],
                recv.at[some_rows(slab, step)],
                (ens, d),
                chunk_sem.at[step],
            ),
        )
    recv[rows_of(slab, blocks), :] = send[rows_of(slab, blocks), :]

    for load in loads[2:]:
        load.wait()
    row = lax.broadcasted_iota(jnp.int32, (levels, levels), 0)
    col = lax.broadcasted_iota(jnp.int32, (levels, levels), 1)
    row_block = jnp.zeros((levels, levels), jnp.int32)
    col_block = jnp.zeros((levels, levels), jnp.int32)
    for j in range(1, bounds_ref.shape[0] - 1):
        row_block += (row >= bounds_ref[j]).astype(jnp.int32)
        col_block += (col >= bounds_ref[j]).astype(jnp.int32)
    solve_s[...] = jnp.where(row_block == col_block, solve_ref[...], 0.0)
    bias = parts_of(bias_in_ref[...] * 0.5)
    land_w = parts_of(land_weight_ref[...] * 0.5)
    land = land_ref[...].astype(jnp.float32)
    extra_row = lax.broadcasted_iota(jnp.int32, (extra, hidden), 0)
    tail = jnp.zeros((extra, hidden), jnp.float32)
    for k, part in enumerate(bias + land_w):
        tail = jnp.where(extra_row == k, part, tail)
    whole = jnp.concatenate([w_in_ref[...].astype(jnp.float32) * 0.5, tail], axis=0)
    w_aug[...] = whole.T.astype(jnp.bfloat16)
    spread = jnp.concatenate(
        [w_out_ref[...].astype(jnp.float32) * 0.5, jnp.zeros((extra, hidden), jnp.float32)], axis=0
    )
    w_back[...] = spread.T.astype(jnp.bfloat16)
    lon_row = lax.broadcasted_iota(jnp.int32, (extra, lons), 0)
    ones = jnp.where(lon_row < 3, 1.0, jnp.where(lon_row < 6, land, 0.0)).astype(jnp.bfloat16)
    bias_col = jnp.sum(jnp.where(row == col, bias_out_ref[...], 0.0), axis=1, keepdims=True)
    for c in range(chunks):
        here = slice(c * width, (c + 1) * width)
        x_aug[c, levels:, :] = ones[:, here]
        shift[c] = bias_col - target_ref[:, here].astype(jnp.float32)
    dy_s[levels:, :] = jnp.zeros((extra, width), jnp.bfloat16)
    grads[...] = jnp.zeros(grads.shape, jnp.float32)

    def gradient(k, x, dy):
        part = rows_of(k, half)
        grads[k, 0:levels, :] += contract(x, da_s[part, :], ((1,), (1,)))
        grads[k, levels:, :] += contract(dy, z_s[part, :], ((1,), (1,)))

    def to_member(e):
        put(1, back.at[rows_of(e, levels)], back_in.at[rows_of(ens, levels)], (e, slab))

    def column_chunk(step, last):
        c = chunk_of(step)
        wait_bytes(recv.at[pl.ds(0, (slabs - 1) * wide)], chunk_sem.at[step])
        h = jnp.concatenate(
            [recv[pl.ds(c * wide + j, levels, stride=blocks), :] for j in range(wide)], axis=1
        )
        x = contract(solve_s[...], h, ((1,), (0,)), precision=highest).astype(jnp.bfloat16)
        x_aug[c, 0:levels, :] = x
        x_all = x_aug[c]
        for k in range(0, hidden, hb):
            pre = contract(w_aug[k : k + hb, :], x_all, ((1,), (0,)))
            t = jnp.tanh(pre)
            both = pre * t
            z_s[k : k + hb, :] = (pre + both).astype(jnp.bfloat16)
            slope[k : k + hb, :] = (1.0 + t) * (1.0 + pre - both)
        out = contract(w_out_ref[...], z_s[...], ((1,), (0,)))
        dy = ((out + shift[c]) * (1.0 / members)).astype(jnp.bfloat16)
        dy_s[0:levels, :] = dy
        dy_all = dy_s[...]
        for k in range(0, hidden, hb):
            dz = contract(w_back[k : k + hb, :], dy_all, ((1,), (0,)))
            da_s[k : k + hb, :] = (dz * slope[k : k + hb, :]).astype(jnp.bfloat16)
        if last:
            gradient(1 - core, x, dy)
            put(2, grads.at[1 - core], pair_in, (ens, twin))
        dx = contract(w_in_ref[...], da_s[...], ((1,), (0,)))
        dh = contract(solve_s[...], dx, ((0,), (0,)), precision=highest)
        for j in range(wide):
            e = c * wide + j
            back[rows_of(e, levels), :] = dh[:, j * LANES : (j + 1) * LANES]
            pl.when(e != ens)(functools.partial(to_member, e))
        if last:
            gradient(core, x, dy)
        else:
            gradient(0, x, dy)
            gradient(1, x, dy)

    def column_step(step, carry):
        column_chunk(step, False)
        return carry

    lax.fori_loop(0, chunks - 1, column_step, 0)
    column_chunk(chunks - 1, True)
    back_in[rows_of(ens, levels), :] = back[rows_of(ens, levels), :]
    wait_bytes(pair_in, recv_sem.at[2])
    pair_sum[...] = grads[core] + pair_in[...]

    def plane_device(q):
        return (q // 2, lax.rem(q, 2) * half_slabs + column)

    for_peers(
        planes,
        plane,
        lambda q: put(
            3, pair_sum.at[rows_of(q, rows)], plane_in.at[rows_of(plane, rows)], plane_device(q)
        ),
    )
    plane_in[rows_of(plane, rows), :] = pair_sum[rows_of(plane, rows), :]
    wait_bytes(back_in.at[pl.ds(0, (members - 1) * levels)], recv_sem.at[1])
    summed = back_in[0:levels, :]
    for e in range(1, members):
        summed += back_in[e * levels : (e + 1) * levels, :]
    level_out[...] = summed
    for_peers(
        slabs,
        slab,
        lambda d: put(4, level_out.at[pl.ds(d, 1)], level_in.at[pl.ds(slab, 1)], (ens, d)),
    )
    level_in[pl.ds(slab, 1), :] = level_out[pl.ds(slab, 1), :]
    wait_bytes(plane_in.at[pl.ds(0, (planes - 1) * rows)], recv_sem.at[3])
    summed = plane_in[0:rows, :]
    for q in range(1, planes):
        summed += plane_in[q * rows : (q + 1) * rows, :]

    def height_device(h):
        return (ens, upper * half_slabs + 2 * h + core)

    spot, group = lax.rem(height, near), height // near
    near_in[rows_of(spot, rows), :] = summed
    mine = rows_of(spot, rows)
    for k in range(1, near):
        peer = group * near + lax.rem(spot + k, near)
        put(5, near_in.at[mine], near_in.at[mine], height_device(peer))
    wait_bytes(near_in.at[pl.ds(0, (near - 1) * rows)], recv_sem.at[5])
    summed = near_in[0:rows, :]
    for k in range(1, near):
        summed += near_in[k * rows : (k + 1) * rows, :]
    from_far = rows_of(group, rows)
    far_in[from_far, :] = summed
    for k in range(1, far):
        peer = lax.rem(height + k * near, heights)
        put(6, far_in.at[from_far], far_in.at[from_far], height_device(peer))
    wait_bytes(level_in.at[pl.ds(0, slabs - 1)], recv_sem.at[4])
    for_peers(
        members, ens, lambda e: put(7, level_in, field_in.at[rows_of(ens, lats)], (e, slab))
    )
    field_in[rows_of(ens, lats), :] = level_in[...]
    wait_bytes(far_in.at[pl.ds(0, (far - 1) * rows)], recv_sem.at[6])
    summed = far_in[0:rows, :]
    for k in range(1, far):
        summed += far_in[k * rows : (k + 1) * rows, :]
    piece[...] = summed
    for_peers(
        planes,
        plane,
        lambda q: put(
            8, piece, half_all.at[rows_of(plane, rows)], plane_device(q), plane_sem.at[plane]
        ),
    )
    half_all[rows_of(plane, rows), :] = piece[...]

    def to_twin(q):
        at = rows_of(q, rows)
        put(9, half_all.at[at], total_hbm.at[core, at], (ens, twin))
        pltpu.make_async_copy(half_all.at[at], total_hbm.at[core, at], store_sem.at[1]).start()

    to_twin(plane)
    wait_bytes(field_in.at[pl.ds(0, (members - 1) * lats)], recv_sem.at[7])
    for e in range(members):
        field[8 : 8 + lats, e * LANES : (e + 1) * LANES] = field_in[e * lats : (e + 1) * lats, :]

    def emit_state(start, count, value):
        state_in[start : start + count, :] = value

    diffuse(field, coef_ref, north, emit_state)
    store_state = pltpu.make_async_copy(state_in, state_hbm_out, store_sem.at[0])
    store_state.start()

    def forward(q):
        wait_bytes(half_all.at[rows_of(q, rows)], plane_sem.at[q])
        to_twin(q)

    for_peers(planes, plane, forward)
    wait_bytes(send.at[pl.ds(0, (slabs - 1) * blocks)], send_sem.at[0])
    wait_bytes(back.at[pl.ds(0, (members - 1) * levels)], send_sem.at[1])
    wait_bytes(pair_in, send_sem.at[2])
    wait_bytes(plane_in.at[pl.ds(0, (planes - 1) * rows)], send_sem.at[3])
    wait_bytes(level_in.at[pl.ds(0, slabs - 1)], send_sem.at[4])
    wait_bytes(near_in.at[pl.ds(0, (near - 1) * rows)], send_sem.at[5])
    wait_bytes(far_in.at[pl.ds(0, (far - 1) * rows)], send_sem.at[6])
    wait_bytes(field_in.at[pl.ds(0, (members - 1) * lats)], send_sem.at[7])
    wait_bytes(half_all.at[pl.ds(0, (planes - 1) * rows)], send_sem.at[8])
    wait_bytes(half_all, send_sem.at[9])
    store_state.wait()
    wait_bytes(half_all, store_sem.at[1])
    wait_bytes(total_hbm.at[1 - core], recv_sem.at[9])


def finish_kernel(
    total_hbm, grad_hbm, in_hbm, out_hbm, state_hbm, total, done, state, load_sem, store_sem
):
    levels, hidden = in_hbm.shape
    half = hidden // 2
    load_state = pltpu.make_async_copy(grad_hbm, state, load_sem.at[2])
    store_state = pltpu.make_async_copy(state, state_hbm, store_sem.at[2])
    loads = []
    for k in range(2):
        at = pl.ds(k * levels, levels)
        loads.append(pltpu.make_async_copy(total_hbm.at[:, at], total.at[:, at], load_sem.at[k]))
        loads[k].start()
    load_state.start()
    stores = []
    for n, ref in enumerate((in_hbm, out_hbm)):
        first = n * levels
        loads[n].wait()
        square = jnp.zeros((1, 1), jnp.float32)
        for k in range(2):
            grad = total[k, first : first + levels, :]
            square += jnp.sum(jnp.sum(grad * grad, axis=0, keepdims=True), axis=1, keepdims=True)
        scale = 1.0 / jnp.sqrt(square * (1.0 / (levels * hidden)) + 1e-06)
        for k in range(2):
            done[n, :, k * half : (k + 1) * half] = total[k, first : first + levels, :] * scale
        stores.append(pltpu.make_async_copy(done.at[n], ref, store_sem.at[n]))
        stores[n].start()
    load_state.wait()
    store_state.start()
    for store in stores:
        store.wait()
    store_state.wait()


def on_device(
    members,
    slabs,
    state,
    face_coefs,
    codes,
    acoustic_inv,
    bounds,
    land_mask,
    target,
    w_in,
    bias_in,
    land_weight,
    w_out,
    bias_out,
):
    _, lats, lons = state.shape
    levels, hidden = w_in.shape
    blocks = lons // LANES
    f32, bf16 = jnp.float32, jnp.bfloat16
    smem = pl.BlockSpec(memory_space=pltpu.SMEM)
    hbm = pl.BlockSpec(memory_space=pltpu.HBM)
    like = jax.ShapeDtypeStruct
    dma = pltpu.SemaphoreType.DMA
    pad = 2 * levels if levels >= 64 else levels + 16
    width = 2 * LANES
    chunks = lons // width
    half = hidden // 2
    planes = 2 * members
    rows = 2 * levels // planes
    heights = slabs // 4
    near = 4 if heights >= 16 else 2
    far = heights // near
    fetched = (
        state.reshape(lats, lons),
        face_coefs.reshape(2, lats, lons),
        acoustic_inv.reshape(levels, levels),
        land_mask,
        target.reshape(levels, lons),
        w_in,
        bias_in.reshape(1, hidden),
        land_weight.reshape(1, hidden),
        w_out.T,
        bias_out.reshape(1, levels),
    )
    grad_state, total = pl.pallas_call(
        functools.partial(step_kernel, members, slabs),
        out_shape=(like((lats, lons), f32), like((2, 2 * levels, half), f32)),
        in_specs=[hbm] * len(fetched) + [smem, smem],
        out_specs=(hbm, hbm),
        scratch_shapes=[pltpu.VMEM(v.shape, v.dtype) for v in fetched]
        + [
            pltpu.VMEM((lats + 16, lons), f32),
            pltpu.VMEM((lats + 8, lons), f32),
            pltpu.VMEM((lats * blocks, LANES), f32),
            pltpu.VMEM((levels * blocks, LANES), f32),
            pltpu.VMEM((levels, levels), f32),
            pltpu.VMEM((hidden, pad), bf16),
            pltpu.VMEM((hidden, pad), bf16),
            pltpu.VMEM((chunks, pad, width), bf16),
            pltpu.VMEM((chunks, levels, width), f32),
            pltpu.VMEM((hidden, width), bf16),
            pltpu.VMEM((hidden, width), f32),
            pltpu.VMEM((pad, width), bf16),
            pltpu.VMEM((hidden, width), bf16),
            pltpu.VMEM((members * levels, LANES), f32),
            pltpu.VMEM((members * levels, LANES), f32),
            pltpu.VMEM((2, 2 * levels, half), f32),
            pltpu.VMEM((2 * levels, half), f32),
            pltpu.VMEM((2 * levels, half), f32),
            pltpu.VMEM((planes * rows, half), f32),
            pltpu.VMEM((near * rows, half), f32),
            pltpu.VMEM((far * rows, half), f32),
            pltpu.VMEM((rows, half), f32),
            pltpu.VMEM((levels, LANES), f32),
            pltpu.VMEM((lats, LANES), f32),
            pltpu.VMEM((members * lats, LANES), f32),
            pltpu.VMEM((2 * levels, half), f32),
            dma((len(fetched),)),
            dma((2,)),
            dma((chunks,)),
            dma((planes,)),
            dma((10,)),
            dma((10,)),
        ],
        compiler_params=pltpu.CompilerParams(
            collective_id=0, has_side_effects=True, vmem_limit_bytes=56 * 1024 * 1024
        ),
    )(*fetched, codes, bounds)
    upd_in, upd_out, grad_state = pl.pallas_call(
        finish_kernel,
        out_shape=(
            like((levels, hidden), f32),
            like((levels, hidden), f32),
            like((lats, lons), f32),
        ),
        in_specs=[hbm] * 2,
        out_specs=(hbm,) * 3,
        scratch_shapes=[
            pltpu.VMEM((2, 2 * levels, half), f32),
            pltpu.VMEM((2, levels, hidden), f32),
            pltpu.VMEM((lats, lons), f32),
            dma((3,)),
            dma((3,)),
        ],
        compiler_params=pltpu.CompilerParams(vmem_limit_bytes=56 * 1024 * 1024),
    )(total, grad_state)
    return upd_in, upd_out.T, grad_state.reshape(state.shape)


def solution(mesh):
    placed = (
        P("slab", None, None),
        P(None, "slab", None, None),
        P("ens"),
        P("slab", None, None),
        P(),
        P("slab", None),
        P(None, "slab", None),
        P(),
        P(),
        P(),
        P(),
        P(),
    )
    return jax.shard_map(
        functools.partial(on_device, mesh.shape["ens"], mesh.shape["slab"]),
        mesh=mesh,
        in_specs=placed,
        out_specs=(P(), P(), P("slab", None, None)),
        check_vma=False,
    )
```

```python
import functools

import jax
import jax.numpy as jnp
from jax import lax
from jax.experimental import pallas as pl
from jax.experimental.pallas import tpu as pltpu
from jax.sharding import PartitionSpec as P

MESH = pl.DeviceIdType.MESH
LANES = 128
PRIME = 65521


def reduced(value):
    value = (value & 65535) + 15 * (value >> 16)
    return value


def below_prime(value):
    return jnp.where(value >= PRIME, value - PRIME, value)


def noise(mult, base, first_row, rows, lons):
    shape = (rows, lons)
    row = lax.broadcasted_iota(jnp.int32, shape, 0) + first_row
    cell = below_prime(row * lons + lax.broadcasted_iota(jnp.int32, shape, 1) + base)
    first = below_prime(reduced(mult * cell + 12345))
    second = below_prime(reduced(reduced(first * 31337 + mult)))
    return second.astype(jnp.float32) * (1.0 / PRIME) - 0.5


def prepare_north(coef_ref, north):
    lats, lons = coef_ref.shape[1:]
    north[0:8, :] = jnp.zeros((8, lons), jnp.float32)
    for start in range(0, lats, 16):
        part = coef_ref[1, start : start + 16, :].astype(jnp.float32)
        if start + 16 >= lats:
            row = lax.broadcasted_iota(jnp.int32, part.shape, 0) + start
            part = jnp.where(row < lats - 1, part, 0.0)
        north[8 + start : 8 + start + part.shape[0], :] = part


def diffuse(field, coef_ref, north, emit):
    lats, lons = coef_ref.shape[1:]
    step = min(16, lats)
    for start in range(0, lats, step):
        here = field[8 + start : 8 + start + step, :]
        ahead = field[9 + start : 9 + start + step, :]
        behind = field[7 + start : 7 + start + step, :]
        east = coef_ref[0, start : start + step, :].astype(jnp.float32)
        flux_x = east * (pltpu.roll(here, lons - 1, 1) - here)
        flux_y = north[8 + start : 8 + start + step, :] * (ahead - here)
        lower = north[7 + start : 7 + start + step, :] * (here - behind)
        emit(start, step, here + flux_x - pltpu.roll(flux_x, 1, 1) + flux_y - lower)


def for_peers(count, me, body):
    far = count // 2
    body(lax.rem(me + far, count))

    def both(step, carry):
        body(lax.rem(me + (far - step), count))
        body(lax.rem(me + (far + step), count))
        return carry

    lax.fori_loop(1, far, both, 0)


def wait_bytes(ref, sem):
    pltpu.make_async_copy(ref, ref, sem).wait()


def rows_of(index, size):
    return pl.ds(pl.multiple_of(index * size, size), size)


def parts_of(value):
    high = value.astype(jnp.bfloat16).astype(jnp.float32)
    rest = value - high
    middle = rest.astype(jnp.bfloat16).astype(jnp.float32)
    return high, middle, rest - middle


def contract(a, b, dims, **kw):
    return lax.dot_general(a, b, (dims, ((), ())), preferred_element_type=jnp.float32, **kw)


def step_kernel(
    members,
    slabs,
    state_hbm,
    coef_hbm,
    solve_hbm,
    land_hbm,
    target_hbm,
    w_in_hbm,
    bias_in_hbm,
    land_weight_hbm,
    w_out_hbm,
    bias_out_hbm,
    code_ref,
    bounds_ref,
    state_hbm_out,
    total_hbm,
    state_in,
    coef_ref,
    solve_ref,
    land_ref,
    target_ref,
    w_in_ref,
    bias_in_ref,
    land_weight_ref,
    w_out_ref,
    bias_out_ref,
    field,
    north,
    send,
    recv,
    solve_s,
    w_aug,
    w_back,
    x_aug,
    shift,
    z_s,
    slope,
    dy_s,
    da_s,
    back,
    back_in,
    grads,
    pair_in,
    pair_sum,
    plane_in,
    near_in,
    far_in,
    piece,
    level_out,
    level_in,
    field_in,
    half_all,
    load_sem,
    store_sem,
    chunk_sem,
    plane_sem,
    send_sem,
    recv_sem,
):
    ens, slab = lax.axis_index("ens"), lax.axis_index("slab")
    lats, lons = state_in.shape
    levels, hidden = w_in_ref.shape
    blocks = lons // LANES
    chunks, pad, width = x_aug.shape
    wide = width // LANES
    extra = pad - levels
    hb = min(128, hidden)
    core = lax.rem(slab, 2)
    twin = slab + 1 - 2 * core
    half_slabs = slabs // 2
    upper = slab // half_slabs
    other = lax.rem(slab + half_slabs, slabs)
    column = lax.rem(slab, half_slabs)
    near = near_in.shape[0] // piece.shape[0]
    far = far_in.shape[0] // piece.shape[0]
    heights = near * far
    height = column // 2
    plane = ens * 2 + upper
    planes = members * 2
    rows = piece.shape[0]
    half = hidden // 2
    highest = lax.Precision.HIGHEST

    loads = [
        pltpu.make_async_copy(src, dst, load_sem.at[k])
        for k, (src, dst) in enumerate(
            (
                (state_hbm, state_in),
                (coef_hbm, coef_ref),
                (solve_hbm, solve_ref),
                (land_hbm, land_ref),
                (target_hbm, target_ref),
                (w_in_hbm, w_in_ref),
                (bias_in_hbm, bias_in_ref),
                (land_weight_hbm, land_weight_ref),
                (w_out_hbm, w_out_ref),
                (bias_out_hbm, bias_out_ref),
            )
        )
    ]
    for load in loads:
        load.start()

    barrier = pltpu.get_barrier_semaphore()

    def greet(device):
        pl.semaphore_signal(barrier, inc=1, device_id=device, device_id_type=MESH)

    def greet_member(e):
        greet((e, slab))
        greet((e, other))

    for_peers(slabs, slab, lambda d: greet((ens, d)))
    for_peers(members, ens, greet_member)

    def put(k, src, dst, device, arrived=None):
        pltpu.make_async_remote_copy(
            src_ref=src,
            dst_ref=dst,
            send_sem=send_sem.at[k],
            recv_sem=recv_sem.at[k] if arrived is None else arrived,
            device_id=device,
            device_id_type=MESH,
        ).start()

    mult = lax.rem(code_ref[0], 251) + 2
    base = lax.rem(slab * (lats * lons), PRIME)
    field[0:8, :] = jnp.zeros((8, lons), jnp.float32)
    field[8 + lats : 16 + lats, :] = jnp.zeros((8, lons), jnp.float32)
    loads[0].wait()
    for start in range(0, lats, 8):
        field[8 + start : 16 + start, :] = state_in[start : start + 8, :] + noise(
            mult, base, start, 8, lons
        )
    loads[1].wait()
    prepare_north(coef_ref, north)

    def emit_send(start, count, value):
        for j in range(blocks):
            send[pl.ds(start * blocks + j, count, stride=blocks), :] = value[
                :, j * LANES : (j + 1) * LANES
            ]

    diffuse(field, coef_ref, north, emit_send)

    def chunk_of(step):
        return lax.rem(ens // 2 + 1 + step, chunks)

    def some_rows(device, step):
        return pl.ds(device * blocks + chunk_of(step) * wide, wide)

    for load in loads[2:]:
        load.wait()
    row = lax.broadcasted_iota(jnp.int32, (levels, levels), 0)
    col = lax.broadcasted_iota(jnp.int32, (levels, levels), 1)
    row_block = jnp.zeros((levels, levels), jnp.int32)
    col_block = jnp.zeros((levels, levels), jnp.int32)
    for j in range(1, bounds_ref.shape[0] - 1):
        row_block += (row >= bounds_ref[j]).astype(jnp.int32)
        col_block += (col >= bounds_ref[j]).astype(jnp.int32)
    solve_s[...] = jnp.where(row_block == col_block, solve_ref[...], 0.0)
    bias = parts_of(bias_in_ref[...] * 0.5)
    land_w = parts_of(land_weight_ref[...] * 0.5)
    land = land_ref[...].astype(jnp.float32)
    extra_row = lax.broadcasted_iota(jnp.int32, (extra, hidden), 0)
    tail = jnp.zeros((extra, hidden), jnp.float32)
    for k, part in enumerate(bias + land_w):
        tail = jnp.where(extra_row == k, part, tail)
    whole = jnp.concatenate([w_in_ref[...].astype(jnp.float32) * 0.5, tail], axis=0)
    w_aug[...] = whole.T.astype(jnp.bfloat16)
    spread = jnp.concatenate(
        [w_out_ref[...].astype(jnp.float32) * 0.5, jnp.zeros((extra, hidden), jnp.float32)], axis=0
    )
    w_back[...] = spread.T.astype(jnp.bfloat16)
    lon_row = lax.broadcasted_iota(jnp.int32, (extra, lons), 0)
    ones = jnp.where(lon_row < 3, 1.0, jnp.where(lon_row < 6, land, 0.0)).astype(jnp.bfloat16)
    bias_col = jnp.sum(jnp.where(row == col, bias_out_ref[...], 0.0), axis=1, keepdims=True)
    for c in range(chunks):
        here = slice(c * width, (c + 1) * width)
        x_aug[c, levels:, :] = ones[:, here]
        shift[c] = bias_col - target_ref[:, here].astype(jnp.float32)
    dy_s[levels:, :] = jnp.zeros((extra, width), jnp.bfloat16)
    grads[...] = jnp.zeros(grads.shape, jnp.float32)

    pl.semaphore_wait(barrier, slabs - 1 + 2 * (members - 1))
    for step in range(chunks):
        for_peers(
            slabs,
            slab,
            lambda d: put(
                0,
                send.at[some_rows(d, step)],
                recv.at[some_rows(slab, step)],
                (ens, d),
                chunk_sem.at[step],
            ),
        )
    recv[rows_of(slab, blocks), :] = send[rows_of(slab, blocks), :]

    def gradient(k, x, dy):
        part = rows_of(k, half)
        grads[k, 0:levels, :] += contract(x, da_s[part, :], ((1,), (1,)))
        grads[k, levels:, :] += contract(dy, z_s[part, :], ((1,), (1,)))

    def to_member(e):
        put(1, back.at[rows_of(e, levels)], back_in.at[rows_of(ens, levels)], (e, slab))

    def column_chunk(step, last):
        c = chunk_of(step)
        wait_bytes(recv.at[pl.ds(0, (slabs - 1) * wide)], chunk_sem.at[step])
        h = jnp.concatenate(
            [recv[pl.ds(c * wide + j, levels, stride=blocks), :] for j in range(wide)], axis=1
        )
        x = contract(solve_s[...], h, ((1,), (0,)), precision=highest).astype(jnp.bfloat16)
        x_aug[c, 0:levels, :] = x
        x_all = x_aug[c]
        for k in range(0, hidden, hb):
            pre = contract(w_aug[k : k + hb, :], x_all, ((1,), (0,)))
            t = jnp.tanh(pre)
            both = pre * t
            z_s[k : k + hb, :] = (pre + both).astype(jnp.bfloat16)
            slope[k : k + hb, :] = (1.0 + t) * (1.0 + pre - both)
        out = contract(w_out_ref[...], z_s[...], ((1,), (0,)))
        dy = ((out + shift[c]) * (1.0 / members)).astype(jnp.bfloat16)
        dy_s[0:levels, :] = dy
        dy_all = dy_s[...]
        for k in range(0, hidden, hb):
            dz = contract(w_back[k : k + hb, :], dy_all, ((1,), (0,)))
            da_s[k : k + hb, :] = (dz * slope[k : k + hb, :]).astype(jnp.bfloat16)
        if last:
            gradient(1 - core, x, dy)
            put(2, grads.at[1 - core], pair_in, (ens, twin))
        dx = contract(w_in_ref[...], da_s[...], ((1,), (0,)))
        dh = contract(solve_s[...], dx, ((0,), (0,)), precision=highest)
        for j in range(wide):
            e = c * wide + j
            back[rows_of(e, levels), :] = dh[:, j * LANES : (j + 1) * LANES]
            pl.when(e != ens)(functools.partial(to_member, e))
        if last:
            gradient(core, x, dy)
        else:
            gradient(0, x, dy)
            gradient(1, x, dy)

    def column_step(step, carry):
        column_chunk(step, False)
        return carry

    lax.fori_loop(0, chunks - 1, column_step, 0)
    column_chunk(chunks - 1, True)
    back_in[rows_of(ens, levels), :] = back[rows_of(ens, levels), :]
    wait_bytes(pair_in, recv_sem.at[2])
    pair_sum[...] = grads[core] + pair_in[...]

    def plane_device(q):
        return (q // 2, lax.rem(q, 2) * half_slabs + column)

    for_peers(
        planes,
        plane,
        lambda q: put(
            3, pair_sum.at[rows_of(q, rows)], plane_in.at[rows_of(plane, rows)], plane_device(q)
        ),
    )
    plane_in[rows_of(plane, rows), :] = pair_sum[rows_of(plane, rows), :]
    wait_bytes(back_in.at[pl.ds(0, (members - 1) * levels)], recv_sem.at[1])
    summed = back_in[0:levels, :]
    for e in range(1, members):
        summed += back_in[e * levels : (e + 1) * levels, :]
    level_out[...] = summed
    for_peers(
        slabs,
        slab,
        lambda d: put(4, level_out.at[pl.ds(d, 1)], level_in.at[pl.ds(slab, 1)], (ens, d)),
    )
    level_in[pl.ds(slab, 1), :] = level_out[pl.ds(slab, 1), :]
    wait_bytes(plane_in.at[pl.ds(0, (planes - 1) * rows)], recv_sem.at[3])
    summed = plane_in[0:rows, :]
    for q in range(1, planes):
        summed += plane_in[q * rows : (q + 1) * rows, :]

    def height_device(h):
        return (ens, upper * half_slabs + 2 * h + core)

    spot, group = lax.rem(height, near), height // near
    near_in[rows_of(spot, rows), :] = summed
    mine = rows_of(spot, rows)
    for k in range(1, near):
        peer = group * near + lax.rem(spot + k, near)
        put(5, near_in.at[mine], near_in.at[mine], height_device(peer))
    wait_bytes(near_in.at[pl.ds(0, (near - 1) * rows)], recv_sem.at[5])
    summed = near_in[0:rows, :]
    for k in range(1, near):
        summed += near_in[k * rows : (k + 1) * rows, :]
    from_far = rows_of(group, rows)
    far_in[from_far, :] = summed
    for k in range(1, far):
        peer = lax.rem(height + k * near, heights)
        put(6, far_in.at[from_far], far_in.at[from_far], height_device(peer))
    wait_bytes(level_in.at[pl.ds(0, slabs - 1)], recv_sem.at[4])
    for_peers(
        members, ens, lambda e: put(7, level_in, field_in.at[rows_of(ens, lats)], (e, slab))
    )
    field_in[rows_of(ens, lats), :] = level_in[...]
    wait_bytes(far_in.at[pl.ds(0, (far - 1) * rows)], recv_sem.at[6])
    summed = far_in[0:rows, :]
    for k in range(1, far):
        summed += far_in[k * rows : (k + 1) * rows, :]
    piece[...] = summed
    for_peers(
        planes,
        plane,
        lambda q: put(
            8, piece, half_all.at[rows_of(plane, rows)], plane_device(q), plane_sem.at[plane]
        ),
    )
    half_all[rows_of(plane, rows), :] = piece[...]

    def to_twin(q):
        at = rows_of(q, rows)
        put(9, half_all.at[at], total_hbm.at[core, at], (ens, twin))
        pltpu.make_async_copy(half_all.at[at], total_hbm.at[core, at], store_sem.at[1]).start()

    to_twin(plane)
    wait_bytes(field_in.at[pl.ds(0, (members - 1) * lats)], recv_sem.at[7])
    for e in range(members):
        field[8 : 8 + lats, e * LANES : (e + 1) * LANES] = field_in[e * lats : (e + 1) * lats, :]

    def emit_state(start, count, value):
        state_in[start : start + count, :] = value

    diffuse(field, coef_ref, north, emit_state)
    store_state = pltpu.make_async_copy(state_in, state_hbm_out, store_sem.at[0])
    store_state.start()

    def forward(q):
        wait_bytes(half_all.at[rows_of(q, rows)], plane_sem.at[q])
        to_twin(q)

    for_peers(planes, plane, forward)
    wait_bytes(send.at[pl.ds(0, (slabs - 1) * blocks)], send_sem.at[0])
    wait_bytes(back.at[pl.ds(0, (members - 1) * levels)], send_sem.at[1])
    wait_bytes(pair_in, send_sem.at[2])
    wait_bytes(plane_in.at[pl.ds(0, (planes - 1) * rows)], send_sem.at[3])
    wait_bytes(level_in.at[pl.ds(0, slabs - 1)], send_sem.at[4])
    wait_bytes(near_in.at[pl.ds(0, (near - 1) * rows)], send_sem.at[5])
    wait_bytes(far_in.at[pl.ds(0, (far - 1) * rows)], send_sem.at[6])
    wait_bytes(field_in.at[pl.ds(0, (members - 1) * lats)], send_sem.at[7])
    wait_bytes(half_all.at[pl.ds(0, (planes - 1) * rows)], send_sem.at[8])
    wait_bytes(half_all, send_sem.at[9])
    store_state.wait()
    wait_bytes(half_all, store_sem.at[1])
    wait_bytes(total_hbm.at[1 - core], recv_sem.at[9])


def finish_kernel(
    total_hbm, grad_hbm, in_hbm, out_hbm, state_hbm, total, done, state, load_sem, store_sem
):
    levels, hidden = in_hbm.shape
    half = hidden // 2
    load_state = pltpu.make_async_copy(grad_hbm, state, load_sem.at[2])
    store_state = pltpu.make_async_copy(state, state_hbm, store_sem.at[2])
    loads = []
    for k in range(2):
        at = pl.ds(k * levels, levels)
        loads.append(pltpu.make_async_copy(total_hbm.at[:, at], total.at[:, at], load_sem.at[k]))
        loads[k].start()
    load_state.start()
    stores = []
    for n, ref in enumerate((in_hbm, out_hbm)):
        first = n * levels
        loads[n].wait()
        square = jnp.zeros((1, 1), jnp.float32)
        for k in range(2):
            grad = total[k, first : first + levels, :]
            square += jnp.sum(jnp.sum(grad * grad, axis=0, keepdims=True), axis=1, keepdims=True)
        scale = 1.0 / jnp.sqrt(square * (1.0 / (levels * hidden)) + 1e-06)
        for k in range(2):
            done[n, :, k * half : (k + 1) * half] = total[k, first : first + levels, :] * scale
        stores.append(pltpu.make_async_copy(done.at[n], ref, store_sem.at[n]))
        stores[n].start()
    load_state.wait()
    store_state.start()
    for store in stores:
        store.wait()
    store_state.wait()


def on_device(
    members,
    slabs,
    state,
    face_coefs,
    codes,
    acoustic_inv,
    bounds,
    land_mask,
    target,
    w_in,
    bias_in,
    land_weight,
    w_out,
    bias_out,
):
    _, lats, lons = state.shape
    levels, hidden = w_in.shape
    blocks = lons // LANES
    f32, bf16 = jnp.float32, jnp.bfloat16
    smem = pl.BlockSpec(memory_space=pltpu.SMEM)
    hbm = pl.BlockSpec(memory_space=pltpu.HBM)
    like = jax.ShapeDtypeStruct
    dma = pltpu.SemaphoreType.DMA
    pad = 2 * levels if levels >= 64 else levels + 16
    width = 2 * LANES
    chunks = lons // width
    half = hidden // 2
    planes = 2 * members
    rows = 2 * levels // planes
    heights = slabs // 4
    near = 4 if heights >= 16 else 2
    far = heights // near
    fetched = (
        state.reshape(lats, lons),
        face_coefs.reshape(2, lats, lons),
        acoustic_inv.reshape(levels, levels),
        land_mask,
        target.reshape(levels, lons),
        w_in,
        bias_in.reshape(1, hidden),
        land_weight.reshape(1, hidden),
        w_out.T,
        bias_out.reshape(1, levels),
    )
    grad_state, total = pl.pallas_call(
        functools.partial(step_kernel, members, slabs),
        out_shape=(like((lats, lons), f32), like((2, 2 * levels, half), f32)),
        in_specs=[hbm] * len(fetched) + [smem, smem],
        out_specs=(hbm, hbm),
        scratch_shapes=[pltpu.VMEM(v.shape, v.dtype) for v in fetched]
        + [
            pltpu.VMEM((lats + 16, lons), f32),
            pltpu.VMEM((lats + 8, lons), f32),
            pltpu.VMEM((lats * blocks, LANES), f32),
            pltpu.VMEM((levels * blocks, LANES), f32),
            pltpu.VMEM((levels, levels), f32),
            pltpu.VMEM((hidden, pad), bf16),
            pltpu.VMEM((hidden, pad), bf16),
            pltpu.VMEM((chunks, pad, width), bf16),
            pltpu.VMEM((chunks, levels, width), f32),
            pltpu.VMEM((hidden, width), bf16),
            pltpu.VMEM((hidden, width), f32),
            pltpu.VMEM((pad, width), bf16),
            pltpu.VMEM((hidden, width), bf16),
            pltpu.VMEM((members * levels, LANES), f32),
            pltpu.VMEM((members * levels, LANES), f32),
            pltpu.VMEM((2, 2 * levels, half), f32),
            pltpu.VMEM((2 * levels, half), f32),
            pltpu.VMEM((2 * levels, half), f32),
            pltpu.VMEM((planes * rows, half), f32),
            pltpu.VMEM((near * rows, half), f32),
            pltpu.VMEM((far * rows, half), f32),
            pltpu.VMEM((rows, half), f32),
            pltpu.VMEM((levels, LANES), f32),
            pltpu.VMEM((lats, LANES), f32),
            pltpu.VMEM((members * lats, LANES), f32),
            pltpu.VMEM((2 * levels, half), f32),
            dma((len(fetched),)),
            dma((2,)),
            dma((chunks,)),
            dma((planes,)),
            dma((10,)),
            dma((10,)),
        ],
        compiler_params=pltpu.CompilerParams(
            collective_id=0, has_side_effects=True, vmem_limit_bytes=56 * 1024 * 1024
        ),
    )(*fetched, codes, bounds)
    upd_in, upd_out, grad_state = pl.pallas_call(
        finish_kernel,
        out_shape=(
            like((levels, hidden), f32),
            like((levels, hidden), f32),
            like((lats, lons), f32),
        ),
        in_specs=[hbm] * 2,
        out_specs=(hbm,) * 3,
        scratch_shapes=[
            pltpu.VMEM((2, 2 * levels, half), f32),
            pltpu.VMEM((2, levels, hidden), f32),
            pltpu.VMEM((lats, lons), f32),
            dma((3,)),
            dma((3,)),
        ],
        compiler_params=pltpu.CompilerParams(vmem_limit_bytes=56 * 1024 * 1024),
    )(total, grad_state)
    return upd_in, upd_out.T, grad_state.reshape(state.shape)


def solution(mesh):
    placed = (
        P("slab", None, None),
        P(None, "slab", None, None),
        P("ens"),
        P("slab", None, None),
        P(),
        P("slab", None),
        P(None, "slab", None),
        P(),
        P(),
        P(),
        P(),
        P(),
    )
    return jax.shard_map(
        functools.partial(on_device, mesh.shape["ens"], mesh.shape["slab"]),
        mesh=mesh,
        in_specs=placed,
        out_specs=(P(), P(), P("slab", None, None)),
        check_vma=False,
    )
```
